128 devices in a mesh: ctx: 64 (over z_hi, y, x, core), head: 2 (over z_lo).
Axes of the slice: x: 4, y: 4, z: 4 (z_hi: 2, z_lo: 2; z = z_hi * 2 + z_lo), core: 2. Of those that a mesh axis runs over, the one named last changes fastest.
Arguments:
- q_heads: bfloat16 [128, 24576], P('ctx', 'head'), may hold values from -6 to 6
- w_uk: bfloat16 [128, 128, 512], P('head'), may hold values from -1 to 1
- latent_t: bfloat16 [576, 65536], P(None, 'ctx'), may hold values from -48 to 48
- index_query: bfloat16 [128, 8192], P('ctx', 'head'), may hold values from -48 to 48
- index_key: bfloat16 [65536, 128], P('ctx'), may hold values from -4 to 4
- head_weight: bfloat16 [128, 64], P('ctx', 'head'), may hold values from 0.099609375 to 1
- query_pos: int32 [128], replicated, may hold values from 32768 to 65535
- key_start: int32 [128], replicated, may hold values from 0 to 16383
Outputs:
- grad_index_query: float32 [128, 8192], P('ctx', 'head')
- grad_index_key: float32 [65536, 128], P('ctx')
- grad_head_weight: float32 [128, 64], P('ctx', 'head')
The draws below stay inside these ranges and needn't reach their ends.
All inputs are finite; a program needn't handle non-finite values.
Results may differ from the reference program's by a relative error of at most 0.0035.
Values may be sent and summed in bfloat16 or wider, within the bound.
A program may use at most 192 MiB of HBM per device.

```python
import math
import jax
import jax.numpy as jnp
from jax import lax

MLA_HEADS = 128
LATENT_RANK = 512
ROPE_DIM = 64
NOPE_DIM = 128
INDEX_HEADS = 64
INDEX_DIM = 128
ALL_KEYS = 65536
QUERIES = 128


def attention_parts(key):
    base = jax.random.fold_in(key, 17)
    key_query, key_weight, key_latent = jax.random.split(base, 3)
    width = NOPE_DIM + ROPE_DIM
    queries = jnp.clip(jax.random.normal(key_query, (QUERIES, MLA_HEADS * width), jnp.float32), -6.0, 6.0)
    absorb_weight = jnp.clip(jax.random.normal(key_weight, (MLA_HEADS, NOPE_DIM, LATENT_RANK), jnp.float32) * NOPE_DIM ** (-0.5), -1.0, 1.0)
    latent_all = jnp.clip(jax.random.normal(key_latent, (LATENT_RANK + ROPE_DIM, ALL_KEYS), jnp.float32), -4.0, 4.0)
    return (queries, absorb_weight, latent_all)


def index_parts(key):
    base = jax.random.fold_in(key, 29)
    key_query, key_keys = jax.random.split(base, 2)
    queries = jnp.clip(jax.random.normal(key_query, (QUERIES, INDEX_HEADS * INDEX_DIM), jnp.float32), -6.0, 6.0)
    keys_all = jnp.clip(jax.random.normal(key_keys, (ALL_KEYS, INDEX_DIM), jnp.float32), -4.0, 4.0)
    return (queries, keys_all)


def draw_q_heads(key, part):
    return attention_parts(key)[0].astype(jnp.bfloat16)


def draw_w_uk(key, part):
    return attention_parts(key)[1].astype(jnp.bfloat16)


def draw_latent_t(key, part):
    return attention_parts(key)[2].astype(jnp.bfloat16)


def draw_index_query(key, part):
    return index_parts(key)[0].astype(jnp.bfloat16)


def draw_index_key(key, part):
    return index_parts(key)[1].astype(jnp.bfloat16)


def place_ends(values, key, least, top_value):
    spot = [jax.random.randint(jax.random.fold_in(key, axis), (), 0, length) for axis, length in enumerate(values.shape)]
    main_axis = values.shape.index(max(values.shape))
    next_to = spot[:main_axis] + [(spot[main_axis] + 1) % values.shape[main_axis]] + spot[main_axis + 1:]
    return values.at[tuple(spot)].set(least).at[tuple(next_to)].set(top_value)


def levels(key, dims, cuts, least, high):
    def one(dim, blocks):
        heights = jax.random.uniform(jax.random.fold_in(jax.random.fold_in(key, 6), dim), (blocks,), jnp.float32, least / len(cuts), high / len(cuts))
        return jnp.repeat(jnp.exp(heights), dims[dim] // blocks).reshape((-1,) + (1,) * (len(dims) - dim - 1))

    gain = one(*cuts[0])
    for cut in cuts[1:]:
        gain = gain * one(*cut)
    return gain


def setup_inputs(seed: int = 0) -> dict:
    keys = jax.random.split(jax.random.key(seed), 9)
    return {
        "q_heads": draw_q_heads(jax.random.fold_in(keys[8], 71), 0),
        "w_uk": draw_w_uk(jax.random.fold_in(keys[8], 71), 0),
        "latent_t": draw_latent_t(jax.random.fold_in(keys[8], 71), 0),
        "index_query": draw_index_query(jax.random.fold_in(keys[8], 71), 0),
        "index_key": draw_index_key(jax.random.fold_in(keys[8], 71), 0),
        "head_weight": jnp.clip(jnp.exp(math.log(1.0) - 2.306499 * jax.random.uniform(keys[5], (QUERIES, INDEX_HEADS), jnp.float32) ** levels(keys[5], (QUERIES, INDEX_HEADS), ((0, 64), (1, 2)), -0.2, 0.2)), 0.099609375, 1.0).astype(jnp.bfloat16),
        "query_pos": place_ends(jax.random.randint(keys[6], (QUERIES,), ALL_KEYS // 2, ALL_KEYS), jax.random.fold_in(keys[6], 1), ALL_KEYS // 2, ALL_KEYS - 1).astype(jnp.int32),
        "key_start": place_ends(jax.random.randint(keys[7], (QUERIES,), 0, ALL_KEYS // 4), jax.random.fold_in(keys[7], 1), 0, (ALL_KEYS // 4) - 1).astype(jnp.int32),
    }


masked_score = -1.0e30


def reference(q_heads, w_uk, latent_t, index_query, index_key, head_weight, query_pos, key_start):
    width = NOPE_DIM + ROPE_DIM
    shaped = q_heads.reshape(QUERIES, MLA_HEADS, width)
    folded = jnp.einsum('qhn,hnc->qhc', shaped[:, :, :NOPE_DIM].astype(jnp.float32), w_uk.astype(jnp.float32))
    latent_query = jnp.concatenate([folded.astype(jnp.bfloat16), shaped[:, :, NOPE_DIM:]], axis=2)
    index_blocks = index_query.reshape(QUERIES, INDEX_HEADS, INDEX_DIM)
    index_scale = (INDEX_DIM * INDEX_HEADS) ** -0.5
    score_scale = width ** -0.5
    scaled_weights = head_weight.astype(jnp.float32) * index_scale
    key_ids = jnp.arange(ALL_KEYS, dtype=jnp.int32)

    def one_query(grad_key, row_items):
        latent_row, index_row, weight_row, position, first_key = row_items
        visible = (key_ids >= first_key) & (key_ids <= position)
        raw_scores = jnp.dot(latent_row, latent_t, preferred_element_type=jnp.float32) * score_scale
        scores = jnp.where(visible[None, :], raw_scores, masked_score)
        row_peak = jnp.max(scores, axis=1, keepdims=True)
        powers = jnp.exp(scores - row_peak)
        row_total = jnp.sum(powers, axis=1, keepdims=True)
        target = jnp.sum(powers / row_total, axis=0) / MLA_HEADS
        dotted = jnp.dot(index_row, index_key.T, preferred_element_type=jnp.float32)
        active = jnp.maximum(dotted, 0.0)
        index_total = jnp.sum(active * weight_row[:, None], axis=0)
        index_masked = jnp.where(visible, index_total, masked_score)
        index_peak = jnp.max(index_masked)
        index_powers = jnp.exp(index_masked - index_peak)
        predicted = index_powers / jnp.sum(index_powers)
        misfit = (predicted - target) * ALL_KEYS
        slopes = jnp.where(dotted > 0, misfit[None, :] * weight_row[:, None], 0.0).astype(jnp.bfloat16)
        grad_query = jnp.dot(slopes, index_key, preferred_element_type=jnp.float32)
        grad_weight = jnp.sum(misfit[None, :] * active, axis=1) * index_scale
        grad_key = grad_key + jnp.dot(slopes.T, index_row, preferred_element_type=jnp.float32)
        return grad_key, (grad_query.reshape(-1), grad_weight)

    start_grad = jnp.zeros((ALL_KEYS, INDEX_DIM), jnp.float32)
    grad_key, outputs = lax.scan(one_query, start_grad, (latent_query, index_blocks, scaled_weights, query_pos, key_start))
    return outputs[0], grad_key, outputs[1]
```

```python
import jax
import jax.numpy as jnp
from jax import lax
from jax.experimental import pallas as pl
from jax.experimental.pallas import tpu as pltpu
from jax.sharding import Mesh
from jax.sharding import PartitionSpec as P

NOPE = 128
ROPE = 64
IDIM = 128
CTX = ("zh", "y", "x", "c")
AXES = ("zh", "y", "x", "c", "head")
MESH_ID = pl.DeviceIdType.MESH

HEADS = 64
IHEADS = 32
QUERIES = 128
KEYS = 1024
ALL_KEYS = 65536
PAIRS = HEADS // 2
IPAIRS = IHEADS // 2
LOG2E = 1.4426950408889634
SCORE_K = (NOPE + ROPE) ** -0.5 * LOG2E
INDEX_SCALE = (IDIM * 64) ** -0.5
MASKED = -1.0e30
TCH = 256
CHUNKS = KEYS // TCH
BR = 80
NCOPY = 25

F32 = jnp.float32
BF16 = jnp.bfloat16


def nt(a, b):
    return lax.dot_general(a, b, (((1,), (1,)), ((), ())), preferred_element_type=F32)


def nn(a, b):
    return lax.dot_general(a, b, (((1,), (0,)), ((), ())), preferred_element_type=F32)


def body(
    blk, wuk, lat, key, bounds, rs_out, gk_out,
    g, nst, ost, wv, lext, lq, sc, pm, iqs, wt, ipart, irecv,
    st, r1, s2, r2, s3, r3, tpart, trecv, mis, keyt, gqt, gwt, gkp, gkr,
    rs, rcv, sb, rya, rxb, pa, pb, rxa, ryb, ab, rz,
    wsem, gsend, grecv, hsend, hrecv, tsend, trsem, ksend, krsem,
    s1send, s1recv, s2send, s2recv, s3send, s3recv, csend, crecv, ysend, yrecv, xsend, xrecv,
    x2send, x2recv, y2send, y2recv, zsend, zrecv,
):
    zh, y, x, c, hd = (lax.axis_index(a) for a in AXES)

    def at(zh_=None, y_=None, x_=None, c_=None, hd_=None):
        return (
            zh if zh_ is None else zh_, y if y_ is None else y_, x if x_ is None else x_,
            c if c_ is None else c_, hd if hd_ is None else hd_,
        )

    def remote(src, dst, ss, rsem, dev):
        return pltpu.make_async_remote_copy(
            src_ref=src, dst_ref=dst, send_sem=ss, recv_sem=rsem, device_id=dev, device_id_type=MESH_ID
        )

    g1, g2 = c * 4 + x, zh * 4 + y

    def peer1(k):
        p = lax.rem(g1 + k, 8)
        return p, at(x_=lax.rem(p, 4), c_=p // 4)

    def peer2(k):
        p = lax.rem(g2 + k, 8)
        return p, at(zh_=p // 4, y_=lax.rem(p, 4))

    barrier = pltpu.get_barrier_semaphore()
    for k in range(1, 8):
        pl.semaphore_signal(barrier, inc=1, device_id=peer1(k)[1], device_id_type=MESH_ID)
        pl.semaphore_signal(barrier, inc=1, device_id=peer2(k)[1], device_id_type=MESH_ID)
    pl.semaphore_signal(barrier, inc=1, device_id=at(hd_=1 - hd), device_id_type=MESH_ID)
    wcopy = pltpu.make_async_copy(wuk, wv, wsem)
    wcopy.start()
    g[c, y, x, zh] = blk[...]
    pl.semaphore_wait(barrier, 15)

    number = iter(range(NCOPY))

    def gcopy(ref, dev):
        k = next(number)
        cp = remote(ref, ref, gsend.at[k], grecv.at[k], dev)
        cp.start()
        return cp

    xr, xl = lax.rem(x + 1, 4), lax.rem(x + 3, 4)
    yr, yl = lax.rem(y + 1, 4), lax.rem(y + 3, 4)
    xo, yo = lax.rem(x + 2, 4), lax.rem(y + 2, 4)
    ra, rb = pl.ds(0, 128), pl.ds(128, 144)
    both, four = pl.ds(0, 2), pl.ds(0, 4)
    lo, hi = pl.ds(0, 2), pl.ds(2, 2)
    other = at(c_=1 - c)
    copies = []
    z0 = gcopy(g.at[c, y, x, zh], at(zh_=1 - zh))
    for a in range(4):
        lext[:, pl.ds(a * 128, 128)] = jnp.transpose(lat[pl.ds(a * 128, 128), :].astype(F32)).astype(BF16)
    rope = lat[pl.ds(512, 64), :].astype(F32)
    lext[:, pl.ds(512, 128)] = jnp.transpose(jnp.concatenate([rope, rope], axis=0)).astype(BF16)
    first = (((zh * 4 + y) * 4 + x) * 2 + c) * KEYS

    def seen(start, rows):
        ids = first + start + lax.broadcasted_iota(jnp.int32, (rows, QUERIES), 0)
        return (ids >= bounds[pl.ds(0, 1), :]) & (ids <= bounds[pl.ds(1, 1), :])

    lext[:, pl.ds(640, 128)] = jnp.where(seen(0, KEYS), 0.0, MASKED).astype(BF16)
    eye = (
        lax.broadcasted_iota(jnp.int32, (128, 128), 0) == lax.broadcasted_iota(jnp.int32, (128, 128), 1)
    ).astype(F32).astype(BF16)
    lq[pl.ds(0, 128), pl.ds(640, 128)] = eye
    lq[pl.ds(128, 128), pl.ds(640, 128)] = eye
    keyt[...] = jnp.transpose(key[...].astype(F32)).astype(BF16)
    z0.wait()
    a1 = gcopy(g.at[c, y, x, both, ra], at(x_=xr)), gcopy(g.at[c, y, x, both, ra], at(x_=xl))
    b1 = gcopy(g.at[c, y, x, both, rb], at(y_=yr)), gcopy(g.at[c, y, x, both, rb], at(y_=yl))
    a1[0].wait_recv()
    a2 = (gcopy(g.at[c, y, xl, 0, ra], at(x_=xr)),)
    b1[0].wait_recv()
    b2 = (gcopy(g.at[c, yl, x, 0, rb], at(y_=yr)),)
    a1[1].wait_recv()
    a2 += (gcopy(g.at[c, y, xr, 1, ra], at(x_=xl)),)
    b1[1].wait_recv()
    b2 += (gcopy(g.at[c, yr, x, 1, rb], at(y_=yl)),)
    a2[0].wait_recv()
    a2[1].wait_recv()
    a3 = (
        gcopy(g.at[c, y, four, both, ra], at(y_=yr)), gcopy(g.at[c, y, four, both, ra], at(y_=yl)),
    )
    copies += [gcopy(g.at[c, y, four, both, ra], other)]
    b2[0].wait_recv()
    b2[1].wait_recv()
    b3 = (
        gcopy(g.at[c, four, x, both, rb], at(x_=xr)), gcopy(g.at[c, four, x, both, rb], at(x_=xl)),
    )
    copies += [gcopy(g.at[c, four, x, both, rb], other)]
    a3[0].wait_recv()
    a4 = (gcopy(g.at[c, yl, lo, both, ra], at(y_=yr)),)
    copies += [gcopy(g.at[c, yl, four, both, ra], other)]
    b3[0].wait_recv()
    b4 = (gcopy(g.at[c, lo, xl, both, rb], at(x_=xr)),)
    copies += [gcopy(g.at[c, four, xl, both, rb], other)]
    a3[1].wait_recv()
    a4 += (gcopy(g.at[c, yr, hi, both, ra], at(y_=yl)),)
    copies += [gcopy(g.at[c, yr, four, both, ra], other)]
    b3[1].wait_recv()
    b4 += (gcopy(g.at[c, hi, xr, both, rb], at(x_=xl)),)
    copies += [gcopy(g.at[c, four, xr, both, rb], other)]
    a4[0].wait_recv()
    a4[1].wait_recv()
    copies += [gcopy(g.at[c, yo, four, both, ra], other)]
    b4[0].wait_recv()
    b4[1].wait_recv()
    copies += [gcopy(g.at[c, four, xo, both, rb], other)]
    for cp in copies:
        cp.wait()
    for cp in a1 + b1 + a2 + b2 + a3 + b3 + a4 + b4:
        cp.wait_send()

    def widen(o, _):
        oc, oy, ox, oz = o // 32, lax.rem(o // 8, 4), lax.rem(o // 2, 4), lax.rem(o, 2)
        nst[pl.ds(pl.multiple_of(o * 128, 128), 128), :] = g[oc, oy, ox, oz, pl.ds(0, 128), :].astype(F32)
        ost[pl.ds(pl.multiple_of(o * 144, 16), 144), :] = g[oc, oy, ox, oz, pl.ds(128, 144), :].astype(F32)
        return 0

    lax.fori_loop(0, 64, widen, 0)

    def rows_of(ref, offset, step, stride):
        return jnp.concatenate(
            [ref[pl.ds(offset + r * step, 64, stride=stride), :] for r in range(2)], axis=0
        )

    wt[...] = jnp.transpose(rows_of(ost, 128, 1, 144)) * INDEX_SCALE

    ipart[...] = jnp.zeros_like(ipart)

    def index_pair(jp, _):
        for e in range(2):
            iqs[jp, pl.ds(e * 128, 128), :] = rows_of(ost, 64 + 2 * jp + e, 32, 144).astype(BF16)
        d = jnp.maximum(nt(key[...], iqs[jp]), 0.0)
        w0, w1 = wt[pl.ds(2 * jp, 1), :], wt[pl.ds(2 * jp + 1, 1), :]
        ipart[...] += d[:, :128] * w0 + d[:, 128:] * w1
        return 0

    lax.fori_loop(0, IPAIRS, index_pair, 0)
    hcopy = remote(ipart, irecv, hsend, hrecv, at(hd_=1 - hd))
    hcopy.start()

    wcopy.wait()
    half = lax.broadcasted_iota(jnp.int32, (128, 128), 1) // 64

    def score_pair(p, _):
        rp = rows_of(ost, p, 32, 144)
        for e in range(2):
            qn = rows_of(nst, 2 * p + e, 64, 128).astype(BF16)
            lq[pl.ds(e * 128, 128), pl.ds(0, 512)] = nn(qn, wv[2 * p + e]).astype(BF16)
            lq[pl.ds(e * 128, 128), pl.ds(512, 128)] = jnp.where(half == e, rp, 0.0).astype(BF16)
        sc[...] = nt(lext[...], lq[...]) * SCORE_K
        t = sc[...]
        m = jnp.max(t, axis=0, keepdims=True)
        pw = jnp.exp2(t - m)
        l = jnp.sum(pw, axis=0, keepdims=True)
        pm[p] = pw.astype(BF16)
        gi, row = p // 4, lax.rem(p, 4) * 2
        for e in range(2):
            st[gi, pl.ds(row + e, 1), :] = m[:, e * 128 : e * 128 + 128]
            st[gi, pl.ds(8 + row + e, 1), :] = l[:, e * 128 : e * 128 + 128]
        return 0

    lax.fori_loop(0, PAIRS, score_pair, 0)

    hcopy.wait()
    it = jnp.where(seen(0, KEYS), (ipart[...] + irecv[...]) * LOG2E, MASKED)
    im = jnp.max(it, axis=0, keepdims=True)
    il = jnp.sum(jnp.exp2(it - im), axis=0, keepdims=True)
    mis[...] = it
    for gi in range(8):
        st[gi, pl.ds(16, 1), :] = im
        st[gi, pl.ds(17, 1), :] = il

    def merged(ref):
        mm = ref[0, pl.ds(0, 8), :]
        jm = ref[0, pl.ds(16, 1), :]
        for k in range(1, 8):
            mm = jnp.maximum(mm, ref[k, pl.ds(0, 8), :])
            jm = jnp.maximum(jm, ref[k, pl.ds(16, 1), :])
        ll, jl = jnp.zeros_like(mm), jnp.zeros_like(jm)
        for k in range(8):
            ll += ref[k, pl.ds(8, 8), :] * jnp.exp2(ref[k, pl.ds(0, 8), :] - mm)
            jl += ref[k, pl.ds(17, 1), :] * jnp.exp2(ref[k, pl.ds(16, 1), :] - jm)
        return mm, ll, jm, jl

    def put(ref, values):
        for at_row, rows, v in zip((0, 8, 16, 17), (8, 8, 1, 1), values):
            ref[pl.ds(at_row, rows), :] = v

    def swap(copies):
        for cp in copies:
            cp.start()
        for cp in copies:
            cp.wait()

    r1[g1] = st[g1]
    cps = []
    for k in range(1, 8):
        p, dev = peer1(k)
        cps.append(remote(st.at[p], r1.at[g1], s1send.at[k], s1recv.at[k], dev))
    swap(cps)
    put(s2, merged(r1))
    r2[g2] = s2[...]
    cps = []
    for k in range(1, 8):
        p, dev = peer2(k)
        cps.append(remote(s2, r2.at[g2], s2send.at[k], s2recv.at[k], dev))
    swap(cps)
    put(s3, merged(r2))
    r3[g1] = s3[...]
    cps = []
    for k in range(1, 8):
        p, dev = peer1(k)
        cps.append(remote(s3, r3.at[g1], s3send.at[k], s3recv.at[k], dev))
    swap(cps)
    for gi in range(8):
        st[gi, pl.ds(0, 8), :] = jnp.exp2(st[gi, pl.ds(0, 8), :] - r3[gi, pl.ds(0, 8), :]) / (
            r3[gi, pl.ds(8, 8), :] * 128.0
        )
    jpeak, jtotal = s3[pl.ds(16, 1), :], s3[pl.ds(17, 1), :]

    tcopies = []
    for ch in range(CHUNKS):
        def add_group(gi, acc, ch=ch):
            for a in range(4):
                pw = pm[gi * 4 + a, pl.ds(ch * TCH, TCH), :].astype(F32)
                acc = acc + pw[:, :128] * st[gi, pl.ds(2 * a, 1), :] + pw[:, 128:] * st[gi, pl.ds(2 * a + 1, 1), :]
            return acc

        rows = pl.ds(ch * TCH, TCH)
        tpart[rows, :] = lax.fori_loop(0, 8, add_group, jnp.zeros((TCH, QUERIES), F32))
        cp = remote(tpart.at[rows], trecv.at[rows], tsend.at[ch], trsem.at[ch], at(hd_=1 - hd))
        cp.start()
        tcopies.append(cp)

    gqt[...] = jnp.zeros_like(gqt)
    gwt[...] = jnp.zeros_like(gwt)
    kcopies = []
    for ch in range(CHUNKS):
        rows = pl.ds(ch * TCH, TCH)
        tcopies[ch].wait()
        predicted = jnp.exp2(mis[rows, :] - jpeak) / jtotal
        mis[rows, :] = (predicted - (tpart[rows, :] + trecv[rows, :])) * ALL_KEYS

        def slope_pair(jp, acc, rows=rows):
            iq = iqs[jp]
            mf = mis[rows, :]
            d = nt(key[rows, :], iq)
            parts = []
            for e in range(2):
                de = d[:, e * 128 : e * 128 + 128]
                gwt[pl.ds(2 * jp + e, 1), :] += jnp.sum(mf * jnp.maximum(de, 0.0), axis=0, keepdims=True)
                parts.append(jnp.where(de > 0, mf * wt[pl.ds(2 * jp + e, 1), :], 0.0).astype(BF16))
            sl = jnp.concatenate(parts, axis=1)
            gqt[jp] += nn(keyt[:, rows], sl)
            return acc + nn(sl, iq)

        gkp[rows, :] = lax.fori_loop(0, IPAIRS, slope_pair, jnp.zeros((TCH, IDIM), F32))
        cp = remote(gkp.at[rows], gkr.at[rows], ksend.at[ch], krsem.at[ch], at(hd_=1 - hd))
        cp.start()
        kcopies.append(cp)

    for j in range(IHEADS):
        tr = jnp.transpose(gqt[j // 2, :, pl.ds((j % 2) * 128, 128)])
        for r in range(2):
            rs[pl.ds(r * 32 + j, 64, stride=BR), :] = tr[r * 64 : r * 64 + 64]
    tw = jnp.transpose(gwt[...]) * INDEX_SCALE
    for r in range(16):
        rs[pl.ds(64 + r, 64, stride=BR), :] = tw[r * 64 : r * 64 + 64] if r < 2 else jnp.zeros((64, 128), F32)

    ccopy = remote(
        rs.at[pl.ds(pl.multiple_of((1 - c) * 32 * BR, BR), 32 * BR)], rcv, csend, crecv, other
    )
    ccopy.start()
    ccopy.wait()

    def add_core(o, _):
        oy, ox, oz = o // 8, lax.rem(o // 2, 4), lax.rem(o, 2)
        here = pl.ds(pl.multiple_of(o * BR, BR), BR)
        v = rcv[here, :] + rs[pl.ds(pl.multiple_of((c * 32 + o) * BR, BR), BR), :]
        rcv[here, :] = v
        w = v[64:72]
        low = w - w.astype(BF16).astype(F32)
        sb[oy, ox, oz] = jnp.concatenate([v[:72], low], axis=0).astype(BF16)
        return 0

    lax.fori_loop(0, 32, add_core, 0)
    cps = []
    for k in range(1, 4):
        yp, xp = lax.rem(y + k, 4), lax.rem(x + k, 4)
        cps.append(remote(sb.at[yp, four, 0], rya.at[k], ysend.at[k], yrecv.at[k], at(y_=yp)))
        cps.append(remote(sb.at[four, xp, 1], rxb.at[k], xsend.at[k], xrecv.at[k], at(x_=xp)))
    swap(cps)

    for o in range(4):
        for dest, src, index in (
            (pa, rya, (y * 4 + o) * 2),
            (pb, rxb, (o * 4 + x) * 2 + 1),
        ):
            v = rcv[pl.ds(pl.multiple_of(index * BR, BR), BR), :]
            main, w = v[:64], v[64:72]
            for k in range(1, 4):
                vk = src[k, o].astype(F32)
                main, w = main + vk[:64], w + (vk[64:72] + vk[72:])
            dest[o, pl.ds(0, 64), :] = main
            dest[o, pl.ds(64, 8), :] = w
            dest[o, pl.ds(72, 8), :] = jnp.zeros((8, 128), F32)
    cps = []
    for k in range(1, 4):
        yp, xp = lax.rem(y + k, 4), lax.rem(x + k, 4)
        cps.append(remote(pa.at[xp], rxa.at[k], x2send.at[k], x2recv.at[k], at(x_=xp)))
        cps.append(remote(pb.at[yp], ryb.at[k], y2send.at[k], y2recv.at[k], at(y_=yp)))
    swap(cps)
    ab[0] = pa[x] + rxa[1] + rxa[2] + rxa[3]
    ab[1] = pb[y] + ryb[1] + ryb[2] + ryb[3]
    swap([remote(ab.at[1 - zh], rz, zsend, zrecv, at(zh_=1 - zh))])
    rs_out[...] = ab[zh] + rz[...]
    for cp in kcopies:
        cp.wait()
    gk_out[...] = gkp[...] + gkr[...]


def shards(q_heads, w_uk, latent_t, index_query, index_key, head_weight, query_pos, key_start):
    shaped = q_heads.reshape(2, HEADS, NOPE + ROPE)
    blk = jnp.concatenate(
        [
            shaped[:, :, :NOPE].reshape(2 * HEADS, 128),
            shaped[:, :, NOPE:].reshape(HEADS, 128),
            index_query.reshape(2 * IHEADS, IDIM),
            jnp.pad(head_weight, ((0, 14), (0, 128 - IHEADS))),
        ],
        axis=0,
    )

    def ordered(v):
        return v.reshape(2, 4, 4, 2, 2).transpose(4, 3, 1, 2, 0).reshape(1, QUERIES)

    bounds = jnp.pad(jnp.concatenate([ordered(key_start), ordered(query_pos)], axis=0), ((0, 6), (0, 0)))
    vm = pl.BlockSpec(memory_space=pltpu.VMEM)
    dma = pltpu.SemaphoreType.DMA

    def v(*shape, dtype=F32):
        return pltpu.VMEM(shape, dtype)

    rs, gk = pl.pallas_call(
        body,
        out_shape=(jax.ShapeDtypeStruct((BR, 128), F32), jax.ShapeDtypeStruct((KEYS, IDIM), F32)),
        in_specs=[vm, pl.BlockSpec(memory_space=pl.ANY), vm, vm, vm],
        out_specs=(vm, vm),
        scratch_shapes=[
            v(2, 4, 4, 2, 272, 128, dtype=BF16),
            v(64 * 128, 128),
            v(64 * 144, 128),
            v(HEADS, NOPE, 512, dtype=BF16),
            v(KEYS, 768, dtype=BF16),
            v(256, 768, dtype=BF16),
            v(KEYS, 256),
            v(PAIRS, KEYS, 256, dtype=BF16),
            v(IPAIRS, 256, 128, dtype=BF16),
            v(128, 128),
            v(KEYS, 128),
            v(KEYS, 128),
            v(8, 24, 128),
            v(8, 24, 128),
            v(24, 128),
            v(8, 24, 128),
            v(24, 128),
            v(8, 24, 128),
            v(KEYS, 128),
            v(KEYS, 128),
            v(KEYS, 128),
            v(128, KEYS, dtype=BF16),
            v(IPAIRS, 128, 256),
            v(128, 128),
            v(KEYS, 128),
            v(KEYS, 128),
            v(64 * BR, 128),
            v(32 * BR, 128),
            v(4, 4, 2, BR, 128, dtype=BF16),
            v(4, 4, BR, 128, dtype=BF16),
            v(4, 4, BR, 128, dtype=BF16),
            v(4, BR, 128),
            v(4, BR, 128),
            v(4, BR, 128),
            v(4, BR, 128),
            v(2, BR, 128),
            v(BR, 128),
            dma, dma((NCOPY,)), dma((NCOPY,)), dma, dma,
            dma((CHUNKS,)), dma((CHUNKS,)), dma((CHUNKS,)), dma((CHUNKS,)),
            dma((8,)), dma((8,)), dma((8,)), dma((8,)), dma((8,)), dma((8,)),
            dma, dma, dma((4,)), dma((4,)), dma((4,)), dma((4,)),
            dma((4,)), dma((4,)), dma((4,)), dma((4,)), dma, dma,
        ],
        compiler_params=pltpu.CompilerParams(
            collective_id=0, has_side_effects=True, vmem_limit_bytes=63 * 1024 * 1024
        ),
    )(blk, w_uk, latent_t, index_key, bounds)
    grad_query = rs[:64].reshape(2, IHEADS * IDIM)
    grad_weight = rs[64:66, :IHEADS]
    return grad_query, gk, grad_weight


def solution(mesh):
    torus = Mesh(mesh.devices.reshape(2, 4, 4, 2, 2), AXES)
    placed = (
        P(CTX, "head"),
        P("head", None, None),
        P(None, CTX),
        P(CTX, "head"),
        P(CTX, None),
        P(CTX, "head"),
        P(),
        P(),
    )
    return jax.shard_map(
        shards,
        mesh=torus,
        in_specs=placed,
        out_specs=(P(CTX, "head"), P(CTX, None), P(CTX, "head")),
        check_vma=False,
    )
```

```python
import jax
import jax.numpy as jnp
from jax import lax
from jax.experimental import pallas as pl
from jax.experimental.pallas import tpu as pltpu
from jax.sharding import Mesh
from jax.sharding import PartitionSpec as P

NOPE = 128
ROPE = 64
IDIM = 128
CTX = ("zh", "y", "x", "c")
AXES = ("zh", "y", "x", "c", "head")
MESH_ID = pl.DeviceIdType.MESH

HEADS = 64
IHEADS = 32
QUERIES = 128
KEYS = 1024
ALL_KEYS = 65536
PAIRS = HEADS // 2
IPAIRS = IHEADS // 2
LOG2E = 1.4426950408889634
SCORE_K = (NOPE + ROPE) ** -0.5 * LOG2E
INDEX_SCALE = (IDIM * 64) ** -0.5
MASKED = -1.0e30
TCH = 256
CHUNKS = KEYS // TCH
BR = 80
NCOPY = 75
UNR = 4
SCH = 256

F32 = jnp.float32
BF16 = jnp.bfloat16


def nt(a, b):
    return lax.dot_general(a, b, (((1,), (1,)), ((), ())), preferred_element_type=F32)


def nn(a, b):
    return lax.dot_general(a, b, (((1,), (0,)), ((), ())), preferred_element_type=F32)


def body(
    qh, iqh, hw, start_in, pos_in, wuk, lat, key, gq_out, gk_out, gw_out,
    raw, low, high, g, hst, ist, wv, lext, lq, lq2, sc, sc2, pm, iqs, wt, ipart, irecv,
    st, r1, s2, r2, s3, r3, tpart, trecv, mis, keyt, gqt, gwt, gkp, gkr,
    rs, rcv, sb, rya, rxb, pab, rz,
    wsem, gsend, grecv, hsend, hrecv, tsend, trsem, ksend, krsem,
    s1send, s1recv, s2send, s2recv, s3send, s3recv, csend, crecv, ysend, yrecv, xsend, xrecv,
    zsend, zrecv,
):
    zh, y, x, c, hd = (lax.axis_index(a) for a in AXES)

    def at(zh_=None, y_=None, x_=None, c_=None, hd_=None):
        return (
            zh if zh_ is None else zh_, y if y_ is None else y_, x if x_ is None else x_,
            c if c_ is None else c_, hd if hd_ is None else hd_,
        )

    def remote(src, dst, ss, rsem, dev):
        return pltpu.make_async_remote_copy(
            src_ref=src, dst_ref=dst, send_sem=ss, recv_sem=rsem, device_id=dev, device_id_type=MESH_ID
        )

    g1, g2 = c * 4 + x, zh * 4 + y

    def peer1(k):
        p = lax.rem(g1 + k, 8)
        return p, at(x_=lax.rem(p, 4), c_=p // 4)

    def peer2(k):
        p = lax.rem(g2 + k, 8)
        return p, at(zh_=p // 4, y_=lax.rem(p, 4))

    barrier = pltpu.get_barrier_semaphore()
    for k in range(1, 8):
        pl.semaphore_signal(barrier, inc=1, device_id=peer1(k)[1], device_id_type=MESH_ID)
        pl.semaphore_signal(barrier, inc=1, device_id=peer2(k)[1], device_id_type=MESH_ID)
    pl.semaphore_signal(barrier, inc=1, device_id=at(hd_=1 - hd), device_id_type=MESH_ID)
    for k in range(1, 4):
        pl.semaphore_signal(
            barrier, inc=1, device_id=at(zh_=1 - zh, x_=lax.rem(x + k, 4)), device_id_type=MESH_ID
        )
    wcopy = pltpu.make_async_copy(wuk, wv, wsem)
    wcopy.start()

    lane = lax.broadcasted_iota(jnp.int32, (2, 128), 1)
    raw[pl.ds(64, 16), :] = jnp.zeros((16, 128), F32)
    for r in range(2):
        raw[pl.ds(64 + r, 1), pl.ds(0, IHEADS)] = hw[pl.ds(r, 1), :].astype(F32)
    for j in range(IHEADS):
        t = iqh[:, pl.ds(j * 128, 128)].astype(F32)
        for r in range(2):
            raw[pl.ds(r * 32 + j, 1), :] = t[r : r + 1]
    for p in range(PAIRS):
        t0, t1, t2 = (qh[:, pl.ds(p * 384 + a * 128, 128)].astype(F32) for a in range(3))
        rope = jnp.where(lane < 64, t1, t2)
        second = pltpu.roll(jnp.where(lane < 64, t2, t1), 64, 1)
        base = 80 + (p // 16) * 96
        hl, pr = (p % 16) * 2, p % 16
        for r in range(2):
            raw[pl.ds(base + r * 32 + hl, 1), :] = t0[r : r + 1]
            raw[pl.ds(base + r * 32 + hl + 1, 1), :] = second[r : r + 1]
            raw[pl.ds(base + 64 + r * 16 + pr, 1), :] = rope[r : r + 1]
    g[c, y, x, zh] = raw[...].astype(BF16)
    qa = lax.broadcasted_iota(jnp.int32, (128, 128), 0)
    qb = lax.broadcasted_iota(jnp.int32, (128, 128), 1)
    place = (
        lax.rem(qb, 2) * 64 + lax.rem(qb // 8, 4) * 16 + lax.rem(qb // 2, 4) * 4 + lax.rem(qb // 32, 2) * 2 + qb // 64
    )
    moved = (qa == place).astype(F32).astype(BF16)

    def ordered(ref):
        v = jnp.broadcast_to(ref[...], (8, 128))
        top = nn((v // 256).astype(F32).astype(BF16), moved)
        rest = nn(lax.rem(v, 256).astype(F32).astype(BF16), moved)
        return (top * 256.0 + rest).astype(jnp.int32)

    low[...] = ordered(start_in)
    high[...] = ordered(pos_in)
    pl.semaphore_wait(barrier, 18)

    number = iter(range(NCOPY))

    def gcopy(ref, dev):
        k = next(number)
        return remote(ref, ref, gsend.at[k], grecv.at[k], dev)

    xr, xl = lax.rem(x + 1, 4), lax.rem(x + 3, 4)
    yr, yl = lax.rem(y + 1, 4), lax.rem(y + 3, 4)
    xo, yo = lax.rem(x + 2, 4), lax.rem(y + 2, 4)
    both, four = pl.ds(0, 2), pl.ds(0, 4)
    front, back = pl.ds(0, 2), pl.ds(2, 2)
    dxr, dxl, dyr, dyl = at(x_=xr), at(x_=xl), at(y_=yr), at(y_=yl)
    other, across = at(c_=1 - c), at(zh_=1 - zh)

    class Piece:
        def __init__(self, row, na, nb):
            ra, rb = pl.ds(row, na), pl.ds(row + na, nb)
            self.z = gcopy(g.at[c, y, x, zh, pl.ds(row, na + nb)], across)
            self.a1 = [gcopy(g.at[c, y, x, both, ra], d) for d in (dxr, dxl)]
            self.b1 = [gcopy(g.at[c, y, x, both, rb], d) for d in (dyr, dyl)]
            self.a2 = [gcopy(g.at[c, y, xl, 0, ra], dxr), gcopy(g.at[c, y, xr, 1, ra], dxl)]
            self.b2 = [gcopy(g.at[c, yl, x, 0, rb], dyr), gcopy(g.at[c, yr, x, 1, rb], dyl)]
            self.a3 = [gcopy(g.at[c, y, four, both, ra], d) for d in (dyr, dyl)]
            self.b3 = [gcopy(g.at[c, four, x, both, rb], d) for d in (dxr, dxl)]
            self.a4 = [gcopy(g.at[c, yl, front, both, ra], dyr), gcopy(g.at[c, yr, back, both, ra], dyl)]
            self.b4 = [gcopy(g.at[c, front, xl, both, rb], dxr), gcopy(g.at[c, back, xr, both, rb], dxl)]
            self.ca = [gcopy(g.at[c, yy, four, both, ra], other) for yy in (y, yl, yr, yo)]
            self.cb = [gcopy(g.at[c, four, xx, both, rb], other) for xx in (x, xl, xr, xo)]

        def step1(self):
            self.z.start()

        def step2(self):
            self.z.wait_recv()
            for cp in self.a1 + self.b1:
                cp.start()

        def step3(self):
            for k in range(2):
                for before, after in ((self.a1, self.a2), (self.b1, self.b2)):
                    before[k].wait_recv()
                    after[k].start()

        def step4(self):
            for before, after, core in ((self.a2, self.a3, self.ca), (self.b2, self.b3, self.cb)):
                for cp in before:
                    cp.wait_recv()
                for cp in after:
                    cp.start()
                core[0].start()

        def step5(self):
            for k in range(2):
                for before, after, core in ((self.a3, self.a4, self.ca), (self.b3, self.b4, self.cb)):
                    before[k].wait_recv()
                    after[k].start()
                    core[1 + k].start()

        def step6(self):
            for before, core in ((self.a4, self.ca), (self.b4, self.cb)):
                for cp in before:
                    cp.wait_recv()
                core[3].start()

        def step7(self):
            for cp in self.ca + self.cb:
                cp.wait()
            for cp in [self.z] + self.a1 + self.b1 + self.a2 + self.b2 + self.a3 + self.b3 + self.a4 + self.b4:
                cp.wait_send()

    first = (((zh * 4 + y) * 4 + x) * 2 + c) * KEYS

    def seen():
        ids = first + lax.broadcasted_iota(jnp.int32, (KEYS, QUERIES), 0)
        return (ids >= low[pl.ds(0, 1), :]) & (ids <= high[pl.ds(0, 1), :])

    def turn(a):
        lext[:, pl.ds(a * 128, 128)] = jnp.transpose(lat[pl.ds(a * 128, 128), :].astype(F32)).astype(BF16)

    p0, p1, p2 = Piece(0, 32, 48), Piece(80, 48, 48), Piece(176, 48, 48)
    p0.step1()
    p1.step1()
    p2.step1()
    lext[:, pl.ds(640, 128)] = jnp.where(seen(), 0.0, MASKED).astype(BF16)
    p0.step2()
    eye = (qa == qb).astype(F32).astype(BF16)
    for ref in (lq, lq2):
        ref[pl.ds(0, 128), pl.ds(640, 128)] = eye
        ref[pl.ds(128, 128), pl.ds(640, 128)] = eye
    p1.step2()
    turn(0)
    p0.step3()
    p2.step2()
    turn(1)
    p0.step4()
    p1.step3()
    turn(2)
    p2.step3()
    p0.step5()
    p1.step4()
    turn(3)
    rope_rows = lat[pl.ds(512, 64), :].astype(F32)
    lext[:, pl.ds(512, 128)] = jnp.transpose(jnp.concatenate([rope_rows, rope_rows], axis=0)).astype(BF16)
    keyt[...] = jnp.transpose(key[...].astype(F32)).astype(BF16)
    p0.step6()
    p0.step7()

    def widened(dest, base, row, rows):
        def one(o, _):
            oc, oy, ox, oz = o // 32, lax.rem(o // 8, 4), lax.rem(o // 2, 4), lax.rem(o, 2)
            dest[pl.ds(pl.multiple_of(base + o * rows, 16), rows), :] = g[oc, oy, ox, oz, pl.ds(row, rows), :].astype(F32)
            return 0

        lax.fori_loop(0, 64, one, 0)

    def rows_of(ref, offset, step, stride):
        return jnp.concatenate(
            [ref[pl.ds(offset + r * step, 64, stride=stride), :] for r in range(2)], axis=0
        )

    widened(ist, 0, 0, 80)
    wt[...] = jnp.transpose(rows_of(ist, 64, 1, 80)) * INDEX_SCALE

    ipart[...] = jnp.zeros_like(ipart)

    def index_pair(jp, _):
        for e in range(2):
            iqs[jp, pl.ds(e * 128, 128), :] = rows_of(ist, 2 * jp + e, 32, 80).astype(BF16)
        d = jnp.maximum(nt(key[...], iqs[jp]), 0.0)
        w0, w1 = wt[pl.ds(2 * jp, 1), :], wt[pl.ds(2 * jp + 1, 1), :]
        ipart[...] += d[:, :128] * w0 + d[:, 128:] * w1
        return 0

    lax.fori_loop(0, IPAIRS // 2, index_pair, 0, unroll=2)
    p1.step5()
    p2.step4()
    lax.fori_loop(IPAIRS // 2, IPAIRS, index_pair, 0, unroll=2)
    hcopy = remote(ipart, irecv, hsend, hrecv, at(hd_=1 - hd))
    hcopy.start()
    p1.step6()
    p2.step5()
    p1.step7()
    widened(hst, 0, 80, 96)

    wcopy.wait()
    half = lax.broadcasted_iota(jnp.int32, (128, 128), 1) // 64

    def prepare(p, dest):
        base = (p // 16) * 6144
        pr = lax.rem(p, 16)
        rp = rows_of(hst, base + 64 + pr, 16, 96)
        for e in range(2):
            qn = rows_of(hst, base + pr * 2 + e, 32, 96).astype(BF16)
            dest[pl.ds(e * 128, 128), pl.ds(0, 512)] = nn(qn, wv[2 * p + e]).astype(BF16)
            dest[pl.ds(e * 128, 128), pl.ds(512, 128)] = jnp.where(half == e, rp, 0.0).astype(BF16)

    def scores(src, dest):
        peak = None
        for a in range(KEYS // SCH):
            t = nt(lext[pl.ds(a * SCH, SCH), :], src[...])
            dest[pl.ds(a * SCH, SCH), :] = t
            top = jnp.max(t.reshape(SCH // 8, 8, 256), axis=0)
            peak = top if peak is None else jnp.maximum(peak, top)
        return jnp.max(peak, axis=0, keepdims=True)

    def powers(p, src, peak):
        total = None
        for a in range(KEYS // SCH):
            pw = jnp.exp2((src[pl.ds(a * SCH, SCH), :] - peak) * SCORE_K)
            pm[p, pl.ds(a * SCH, SCH), :] = pw.astype(BF16)
            part = jnp.sum(pw.reshape(SCH // 8, 8, 256), axis=0)
            total = part if total is None else total + part
        l = jnp.sum(total, axis=0, keepdims=True)
        m = peak * SCORE_K
        part, gi, row = p // 16, lax.rem(p, 16) // 2, lax.rem(p, 2) * 2
        for e in range(2):
            st[part, gi, pl.ds(row + e, 1), :] = m[:, e * 128 : e * 128 + 128]
            st[part, gi, pl.ds(4 + row + e, 1), :] = l[:, e * 128 : e * 128 + 128]

    def merged(ref, part):
        mm = ref[part, 0, pl.ds(0, 4), :]
        jm = ref[part, 0, pl.ds(8, 1), :]
        for k in range(1, 8):
            mm = jnp.maximum(mm, ref[part, k, pl.ds(0, 4), :])
            jm = jnp.maximum(jm, ref[part, k, pl.ds(8, 1), :])
        ll, jl = jnp.zeros_like(mm), jnp.zeros_like(jm)
        for k in range(8):
            ll += ref[part, k, pl.ds(4, 4), :] * jnp.exp2(ref[part, k, pl.ds(0, 4), :] - mm)
            jl += ref[part, k, pl.ds(9, 1), :] * jnp.exp2(ref[part, k, pl.ds(8, 1), :] - jm)
        return mm, ll, jm, jl

    def put(ref, part, values):
        for at_row, rows, v in zip((0, 4, 8, 9), (4, 4, 1, 1), values):
            ref[part, pl.ds(at_row, rows), :] = v

    def begin(copies):
        for cp in copies:
            cp.start()

    def finish(copies):
        for cp in copies:
            cp.wait()

    def swap(copies):
        begin(copies)
        finish(copies)

    class Stats:
        def __init__(self, part):
            self.part = part
            self.c1, self.c2, self.c3 = [], [], []
            for k in range(1, 8):
                p, dev = peer1(k)
                self.c1.append(remote(st.at[part, p], r1.at[part, g1], s1send.at[part, k], s1recv.at[part, k], dev))
                self.c3.append(remote(s3.at[part], r3.at[part, g1], s3send.at[part, k], s3recv.at[part, k], dev))
                p, dev = peer2(k)
                self.c2.append(remote(s2.at[part], r2.at[part, g2], s2send.at[part, k], s2recv.at[part, k], dev))

        def step1(self):
            r1[self.part, g1] = st[self.part, g1]
            begin(self.c1)

        def step2(self):
            finish(self.c1)
            put(s2, self.part, merged(r1, self.part))
            r2[self.part, g2] = s2[self.part]
            begin(self.c2)

        def step3(self):
            finish(self.c2)
            put(s3, self.part, merged(r2, self.part))
            r3[self.part, g1] = s3[self.part]
            begin(self.c3)

        def step4(self):
            finish(self.c3)
            for gi in range(8):
                st[self.part, gi, pl.ds(0, 4), :] = jnp.exp2(
                    st[self.part, gi, pl.ds(0, 4), :] - r3[self.part, gi, pl.ds(0, 4), :]
                ) / (r3[self.part, gi, pl.ds(4, 4), :] * 128.0)

    def index_stats():
        hcopy.wait()
        it = jnp.where(seen(), (ipart[...] + irecv[...]) * LOG2E, MASKED)
        im = jnp.max(it, axis=0, keepdims=True)
        il = jnp.sum(jnp.exp2(it - im), axis=0, keepdims=True)
        mis[...] = it
        for gi in range(8):
            st[0, gi, pl.ds(8, 1), :] = im
            st[0, gi, pl.ds(9, 1), :] = il

    st[...] = jnp.zeros_like(st)
    stats0, stats1 = Stats(0), Stats(1)

    prepare(0, lq)
    peak0 = scores(lq, sc)
    prepare(1, lq2)

    def two_pairs(i, peak):
        p = 2 * i
        peak2 = scores(lq2, sc2)
        prepare(jnp.minimum(p + 2, PAIRS - 1), lq)
        powers(p, sc, peak)
        nxt = scores(lq, sc)
        prepare(jnp.minimum(p + 3, PAIRS - 1), lq2)
        powers(p + 1, sc2, peak2)

        @pl.when(i == 2)
        def _():
            p2.step6()

        @pl.when(i == 6)
        def _():
            p2.step7()
            widened(hst, 6144, 176, 96)

        @pl.when(i == 7)
        def _():
            index_stats()
            stats0.step1()

        @pl.when(i == 10)
        def _():
            stats0.step2()

        @pl.when(i == 12)
        def _():
            stats0.step3()

        @pl.when(i == 15)
        def _():
            stats0.step4()

        return nxt

    lax.fori_loop(0, PAIRS // 2, two_pairs, peak0)

    def add_heads(part, ch, acc):
        def add_group(gi, acc):
            for a in range(2):
                pw = pm[part * 16 + gi * 2 + a, pl.ds(ch * TCH, TCH), :].astype(F32)
                acc = acc + pw[:, :128] * st[part, gi, pl.ds(2 * a, 1), :]
                acc = acc + pw[:, 128:] * st[part, gi, pl.ds(2 * a + 1, 1), :]
            return acc

        return lax.fori_loop(0, 8, add_group, acc, unroll=2)

    def early(chs):
        for ch in chs:
            tpart[pl.ds(ch * TCH, TCH), :] = add_heads(0, ch, jnp.zeros((TCH, QUERIES), F32))

    stats1.step1()
    early(range(0, CHUNKS // 2))
    stats1.step2()
    early(range(CHUNKS // 2, CHUNKS))
    stats1.step3()
    gqt[...] = jnp.zeros_like(gqt)
    gwt[...] = jnp.zeros_like(gwt)
    jpeak, jtotal = s3[0, pl.ds(8, 1), :], s3[0, pl.ds(9, 1), :]
    stats1.step4()

    tcopies = []
    for ch in range(CHUNKS):
        rows = pl.ds(ch * TCH, TCH)
        tpart[rows, :] = add_heads(1, ch, tpart[rows, :])
        cp = remote(tpart.at[rows], trecv.at[rows], tsend.at[ch], trsem.at[ch], at(hd_=1 - hd))
        cp.start()
        tcopies.append(cp)

    kcopies = []
    for ch in range(CHUNKS):
        rows = pl.ds(ch * TCH, TCH)
        tcopies[ch].wait()
        predicted = jnp.exp2(mis[rows, :] - jpeak) / jtotal
        mis[rows, :] = (predicted - (tpart[rows, :] + trecv[rows, :])) * ALL_KEYS

        def slope_pair(jp, acc, rows=rows):
            iq = iqs[jp]
            mf = mis[rows, :]
            d = nt(key[rows, :], iq)
            parts = []
            for e in range(2):
                de = d[:, e * 128 : e * 128 + 128]
                gwt[pl.ds(2 * jp + e, 1), :] += jnp.sum(mf * jnp.maximum(de, 0.0), axis=0, keepdims=True)
                parts.append(jnp.where(de > 0, mf * wt[pl.ds(2 * jp + e, 1), :], 0.0).astype(BF16))
            sl = jnp.concatenate(parts, axis=1)
            gqt[jp] += nn(keyt[:, rows], sl)
            return acc + nn(sl, iq)

        gkp[rows, :] = lax.fori_loop(0, IPAIRS, slope_pair, jnp.zeros((TCH, IDIM), F32), unroll=UNR)
        cp = remote(gkp.at[rows], gkr.at[rows], ksend.at[ch], krsem.at[ch], at(hd_=1 - hd))
        cp.start()
        kcopies.append(cp)

    for j in range(IHEADS):
        tr = jnp.transpose(gqt[j // 2, :, pl.ds((j % 2) * 128, 128)])
        for r in range(2):
            rs[pl.ds(r * 32 + j, 64, stride=BR), :] = tr[r * 64 : r * 64 + 64]
    tw = jnp.transpose(gwt[...]) * INDEX_SCALE
    for r in range(16):
        rs[pl.ds(64 + r, 64, stride=BR), :] = tw[r * 64 : r * 64 + 64] if r < 2 else jnp.zeros((64, 128), F32)

    ccopy = remote(
        rs.at[pl.ds(pl.multiple_of((1 - c) * 32 * BR, BR), 32 * BR)], rcv, csend, crecv, other
    )
    ccopy.start()
    ccopy.wait()

    def add_core(o, _):
        oy, ox, oz = o // 8, lax.rem(o // 2, 4), lax.rem(o, 2)
        here = pl.ds(pl.multiple_of(o * BR, BR), BR)
        v = rcv[here, :] + rs[pl.ds(pl.multiple_of((c * 32 + o) * BR, BR), BR), :]
        rcv[here, :] = v
        w = v[64:72]
        low = w - w.astype(BF16).astype(F32)
        sb[oy, ox, oz] = jnp.concatenate([v[:72], low], axis=0).astype(BF16)
        return 0

    lax.fori_loop(0, 32, add_core, 0)
    cps = []
    for k in range(1, 4):
        yp, xp = lax.rem(y + k, 4), lax.rem(x + k, 4)
        cps.append(remote(sb.at[yp, four, 0], rya.at[k], ysend.at[k], yrecv.at[k], at(y_=yp)))
        cps.append(remote(sb.at[four, xp, 1], rxb.at[k], xsend.at[k], xrecv.at[k], at(x_=xp)))
    swap(cps)

    for o in range(4):
        for dest, src, index in (
            (0, rya, (y * 4 + o) * 2),
            (1, rxb, (o * 4 + x) * 2 + 1),
        ):
            v = rcv[pl.ds(pl.multiple_of(index * BR, BR), BR), :]
            main, w = v[:64], v[64:72]
            for k in range(1, 4):
                vk = src[k, o].astype(F32)
                main, w = main + vk[:64], w + (vk[64:72] + vk[72:])
            pab[dest, o, pl.ds(0, 64), :] = main
            pab[dest, o, pl.ds(64, 8), :] = w
            pab[dest, o, pl.ds(72, 8), :] = jnp.zeros((8, 128), F32)
    mine = x * (1 - zh) + y * zh
    theirs = x * zh + y * (1 - zh)
    rz[zh * 4 + mine] = pab[zh, mine]
    cps = []
    for k in range(1, 4):
        yp, xp = lax.rem(y + k, 4), lax.rem(x + k, 4)
        slot = zh * 4 + x
        cps.append(remote(pab.at[0, xp], rz.at[slot], zsend.at[k], zrecv.at[slot], at(zh_=0, x_=xp)))
        slot = zh * 4 + y
        cps.append(remote(pab.at[1, yp], rz.at[slot], zsend.at[3 + k], zrecv.at[slot], at(zh_=1, y_=yp)))
    slot = zh * 4 + theirs
    cps.append(remote(pab.at[1 - zh, theirs], rz.at[slot], zsend.at[0], zrecv.at[slot], across))
    begin(cps)
    for cp in cps:
        cp.wait_send()
    for k in range(1, 8):
        slot = lax.rem(zh * 4 + mine + k, 8)
        remote(pab.at[0, 0], rz.at[slot], zsend.at[0], zrecv.at[slot], across).wait_recv()
    total = rz[0]
    for k in range(1, 8):
        total = total + rz[k]
    raw[pl.ds(0, BR), :] = total
    for r in range(2):
        for j in range(IHEADS):
            gq_out[pl.ds(r, 1), pl.ds(j * 128, 128)] = raw[pl.ds(r * 32 + j, 1), :]
        gw_out[pl.ds(r, 1), :] = raw[pl.ds(64 + r, 1), pl.ds(0, IHEADS)]
    for cp in kcopies:
        cp.wait()
    gk_out[...] = gkp[...] + gkr[...]


def shards(q_heads, w_uk, latent_t, index_query, index_key, head_weight, query_pos, key_start):
    vm = pl.BlockSpec(memory_space=pltpu.VMEM)
    dma = pltpu.SemaphoreType.DMA

    def v(*shape, dtype=F32):
        return pltpu.VMEM(shape, dtype)

    return pl.pallas_call(
        body,
        out_shape=(
            jax.ShapeDtypeStruct((2, IHEADS * IDIM), F32),
            jax.ShapeDtypeStruct((KEYS, IDIM), F32),
            jax.ShapeDtypeStruct((2, IHEADS), F32),
        ),
        in_specs=[vm, vm, vm, vm, vm, pl.BlockSpec(memory_space=pl.ANY), vm, vm],
        out_specs=(vm, vm, vm),
        scratch_shapes=[
            v(272, 128),
            v(8, 128, dtype=jnp.int32),
            v(8, 128, dtype=jnp.int32),
            v(2, 4, 4, 2, 272, 128, dtype=BF16),
            v(2 * 64 * 96, 128),
            v(64 * 80, 128),
            v(HEADS, NOPE, 512, dtype=BF16),
            v(KEYS, 768, dtype=BF16),
            v(256, 768, dtype=BF16),
            v(256, 768, dtype=BF16),
            v(KEYS, 256),
            v(KEYS, 256),
            v(PAIRS, KEYS, 256, dtype=BF16),
            v(IPAIRS, 256, 128, dtype=BF16),
            v(128, 128),
            v(KEYS, 128),
            v(KEYS, 128),
            v(2, 8, 16, 128),
            v(2, 8, 16, 128),
            v(2, 16, 128),
            v(2, 8, 16, 128),
            v(2, 16, 128),
            v(2, 8, 16, 128),
            v(KEYS, 128),
            v(KEYS, 128),
            v(KEYS, 128),
            v(128, KEYS, dtype=BF16),
            v(IPAIRS, 128, 256),
            v(128, 128),
            v(KEYS, 128),
            v(KEYS, 128),
            v(64 * BR, 128),
            v(32 * BR, 128),
            v(4, 4, 2, BR, 128, dtype=BF16),
            v(4, 4, BR, 128, dtype=BF16),
            v(4, 4, BR, 128, dtype=BF16),
            v(2, 4, BR, 128),
            v(8, BR, 128),
            dma, dma((NCOPY,)), dma((NCOPY,)), dma, dma,
            dma((CHUNKS,)), dma((CHUNKS,)), dma((CHUNKS,)), dma((CHUNKS,)),
            dma((2, 8)), dma((2, 8)), dma((2, 8)), dma((2, 8)), dma((2, 8)), dma((2, 8)),
            dma, dma, dma((4,)), dma((4,)), dma((4,)), dma((4,)),
            dma((8,)), dma((8,)),
        ],
        compiler_params=pltpu.CompilerParams(
            collective_id=0, has_side_effects=True, vmem_limit_bytes=63 * 1024 * 1024
        ),
    )(
        q_heads, index_query, head_weight, key_start.reshape(1, QUERIES), query_pos.reshape(1, QUERIES),
        w_uk, latent_t, index_key,
    )


def solution(mesh):
    torus = Mesh(mesh.devices.reshape(2, 4, 4, 2, 2), AXES)
    placed = (
        P(CTX, "head"),
        P("head", None, None),
        P(None, CTX),
        P(CTX, "head"),
        P(CTX, None),
        P(CTX, "head"),
        P(),
        P(),
    )
    return jax.shard_map(
        shards,
        mesh=torus,
        in_specs=placed,
        out_specs=(P(CTX, "head"), P(CTX, None), P(CTX, "head")),
        check_vma=False,
    )
```

```python
import jax
import jax.numpy as jnp
from jax import lax
from jax.experimental import pallas as pl
from jax.experimental.pallas import tpu as pltpu
from jax.sharding import Mesh
from jax.sharding import PartitionSpec as P

NOPE = 128
ROPE = 64
IDIM = 128
CTX = ("zh", "y", "x", "c")
AXES = ("zh", "y", "x", "c", "head")
MESH_ID = pl.DeviceIdType.MESH

HEADS = 64
IHEADS = 32
QUERIES = 128
KEYS = 1024
ALL_KEYS = 65536
PAIRS = HEADS // 2
IPAIRS = IHEADS // 2
LOG2E = 1.4426950408889634
SCORE_K = (NOPE + ROPE) ** -0.5 * LOG2E
INDEX_SCALE = (IDIM * 64) ** -0.5
MASKED = -1.0e30
TCH = 256
CHUNKS = KEYS // TCH
BR = 80
NCOPY = 84
UNR = 4
SCH = 256

F32 = jnp.float32
BF16 = jnp.bfloat16


def nt(a, b):
    return lax.dot_general(a, b, (((1,), (1,)), ((), ())), preferred_element_type=F32)


def nn(a, b):
    return lax.dot_general(a, b, (((1,), (0,)), ((), ())), preferred_element_type=F32)


def body(
    qh, iqh, hw, start_in, pos_in, wuk, lat, key, gq_out, gk_out, gw_out,
    raw, low, high, g, hst, ist, wv, lext, lq, lq2, sc, sc2, pm, iqs, wt, ipart, irecv,
    st, r1, s2, r2, s3, r3, tpart, trecv, mis, keyt, gqt, gwt, gkp, gkr,
    rs, rcv, sb, rya, rxb, pab, rz,
    wsem, gsend, grecv, hsend, hrecv, tsend, trsem, ksend, krsem,
    s1send, s1recv, s2send, s2recv, s3send, s3recv, csend, crecv, ysend, yrecv, xsend, xrecv,
    zsend, zrecv,
):
    zh, y, x, c, hd = (lax.axis_index(a) for a in AXES)

    def at(zh_=None, y_=None, x_=None, c_=None, hd_=None):
        return (
            zh if zh_ is None else zh_, y if y_ is None else y_, x if x_ is None else x_,
            c if c_ is None else c_, hd if hd_ is None else hd_,
        )

    def remote(src, dst, ss, rsem, dev):
        return pltpu.make_async_remote_copy(
            src_ref=src, dst_ref=dst, send_sem=ss, recv_sem=rsem, device_id=dev, device_id_type=MESH_ID
        )

    g1, g2 = c * 4 + x, zh * 4 + y

    def peer1(k):
        p = lax.rem(g1 + k, 8)
        return p, at(x_=lax.rem(p, 4), c_=p // 4)

    def peer2(k):
        p = lax.rem(g2 + k, 8)
        return p, at(zh_=p // 4, y_=lax.rem(p, 4))

    barrier = pltpu.get_barrier_semaphore()
    for k in range(1, 8):
        pl.semaphore_signal(barrier, inc=1, device_id=peer1(k)[1], device_id_type=MESH_ID)
        pl.semaphore_signal(barrier, inc=1, device_id=peer2(k)[1], device_id_type=MESH_ID)
    pl.semaphore_signal(barrier, inc=1, device_id=at(hd_=1 - hd), device_id_type=MESH_ID)
    for k in range(1, 4):
        pl.semaphore_signal(
            barrier, inc=1, device_id=at(zh_=1 - zh, x_=lax.rem(x + k, 4)), device_id_type=MESH_ID
        )
    wcopy = pltpu.make_async_copy(wuk, wv, wsem)
    wcopy.start()

    lane = lax.broadcasted_iota(jnp.int32, (2, 128), 1)
    raw[pl.ds(64, 16), :] = jnp.zeros((16, 128), F32)
    for r in range(2):
        raw[pl.ds(64 + r, 1), pl.ds(0, IHEADS)] = hw[pl.ds(r, 1), :].astype(F32)
    for j in range(IHEADS):
        t = iqh[:, pl.ds(j * 128, 128)].astype(F32)
        for r in range(2):
            raw[pl.ds(r * 32 + j, 1), :] = t[r : r + 1]
    for p in range(PAIRS):
        t0, t1, t2 = (qh[:, pl.ds(p * 384 + a * 128, 128)].astype(F32) for a in range(3))
        rope = jnp.where(lane < 64, t1, t2)
        second = pltpu.roll(jnp.where(lane < 64, t2, t1), 64, 1)
        base = 80 + (p // 16) * 96
        hl, pr = (p % 16) * 2, p % 16
        for r in range(2):
            raw[pl.ds(base + r * 32 + hl, 1), :] = t0[r : r + 1]
            raw[pl.ds(base + r * 32 + hl + 1, 1), :] = second[r : r + 1]
            raw[pl.ds(base + 64 + r * 16 + pr, 1), :] = rope[r : r + 1]
    g[c, y, x, zh] = raw[...].astype(BF16)
    qa = lax.broadcasted_iota(jnp.int32, (128, 128), 0)
    qb = lax.broadcasted_iota(jnp.int32, (128, 128), 1)
    place = (
        lax.rem(qb, 2) * 64 + lax.rem(qb // 8, 4) * 16 + lax.rem(qb // 2, 4) * 4 + lax.rem(qb // 32, 2) * 2 + qb // 64
    )
    moved = (qa == place).astype(F32).astype(BF16)

    def ordered(ref):
        v = jnp.broadcast_to(ref[...], (8, 128))
        top = nn((v // 256).astype(F32).astype(BF16), moved)
        rest = nn(lax.rem(v, 256).astype(F32).astype(BF16), moved)
        return (top * 256.0 + rest).astype(jnp.int32)

    low[...] = ordered(start_in)
    high[...] = ordered(pos_in)
    pl.semaphore_wait(barrier, 18)

    number = iter(range(NCOPY))

    def gcopy(ref, dev):
        k = next(number)
        return remote(ref, ref, gsend.at[k], grecv.at[k], dev)

    xr, xl = lax.rem(x + 1, 4), lax.rem(x + 3, 4)
    yr, yl = lax.rem(y + 1, 4), lax.rem(y + 3, 4)
    xo, yo = lax.rem(x + 2, 4), lax.rem(y + 2, 4)
    both, four = pl.ds(0, 2), pl.ds(0, 4)
    other, across = at(c_=1 - c), at(zh_=1 - zh)
    near = (1, 3, 2)
    peers_zx = [at(x_=lax.rem(x + k, 4)) for k in near] + [across]
    peers_zx += [at(zh_=1 - zh, x_=lax.rem(x + k, 4)) for k in near]
    peers_zy = [at(y_=lax.rem(y + k, 4)) for k in near] + [across]
    peers_zy += [at(zh_=1 - zh, y_=lax.rem(y + k, 4)) for k in near]

    class Piece:
        def __init__(self, row, na, nb):
            ra, rb = pl.ds(row, na), pl.ds(row + na, nb)
            own_a, own_b = g.at[c, y, x, zh, ra], g.at[c, y, x, zh, rb]
            self.a1 = [gcopy(own_a, d) for d in peers_zx]
            self.b1 = [gcopy(own_b, d) for d in peers_zy]
            self.a2 = [gcopy(g.at[c, y, four, both, ra], at(y_=q)) for q in (yr, yl, yo)]
            self.b2 = [gcopy(g.at[c, four, x, both, rb], at(x_=q)) for q in (xr, xl, xo)]
            self.ca = [gcopy(g.at[c, q, four, both, ra], other) for q in (y, yl, yr, yo)]
            self.cb = [gcopy(g.at[c, four, q, both, rb], other) for q in (x, xl, xr, xo)]

        def step1(self):
            for cp in self.a1 + self.b1:
                cp.start()

        def step2(self):
            for before, after, core in ((self.a1, self.a2, self.ca), (self.b1, self.b2, self.cb)):
                for cp in before:
                    cp.wait_recv()
                for cp in after:
                    cp.start()
                core[0].start()

        def step3(self):
            for k in range(3):
                for before, core in ((self.a2, self.ca), (self.b2, self.cb)):
                    before[k].wait_recv()
                    core[1 + k].start()

        def step4(self):
            for cp in self.ca + self.cb:
                cp.wait()
            for cp in self.a1 + self.b1 + self.a2 + self.b2:
                cp.wait_send()

    first = (((zh * 4 + y) * 4 + x) * 2 + c) * KEYS

    def seen():
        ids = first + lax.broadcasted_iota(jnp.int32, (KEYS, QUERIES), 0)
        return (ids >= low[pl.ds(0, 1), :]) & (ids <= high[pl.ds(0, 1), :])

    def turn(a):
        lext[:, pl.ds(a * 128, 128)] = jnp.transpose(lat[pl.ds(a * 128, 128), :].astype(F32)).astype(BF16)

    p0, p1, p2 = Piece(0, 32, 48), Piece(80, 48, 48), Piece(176, 48, 48)
    p0.step1()
    p1.step1()
    p2.step1()
    lext[:, pl.ds(640, 128)] = jnp.where(seen(), 0.0, MASKED).astype(BF16)
    eye = (qa == qb).astype(F32).astype(BF16)
    for ref in (lq, lq2):
        ref[pl.ds(0, 128), pl.ds(640, 128)] = eye
        ref[pl.ds(128, 128), pl.ds(640, 128)] = eye
    turn(0)
    p0.step2()
    turn(1)
    turn(2)
    turn(3)
    p1.step2()
    rope_rows = lat[pl.ds(512, 64), :].astype(F32)
    lext[:, pl.ds(512, 128)] = jnp.transpose(jnp.concatenate([rope_rows, rope_rows], axis=0)).astype(BF16)
    keyt[...] = jnp.transpose(key[...].astype(F32)).astype(BF16)
    p0.step3()
    p0.step4()

    def widened(dest, base, row, rows):
        def one(o, _):
            oc, oy, ox, oz = o // 32, lax.rem(o // 8, 4), lax.rem(o // 2, 4), lax.rem(o, 2)
            dest[pl.ds(pl.multiple_of(base + o * rows, 16), rows), :] = g[oc, oy, ox, oz, pl.ds(row, rows), :].astype(F32)
            return 0

        lax.fori_loop(0, 64, one, 0)

    def rows_of(ref, offset, step, stride):
        return jnp.concatenate(
            [ref[pl.ds(offset + r * step, 64, stride=stride), :] for r in range(2)], axis=0
        )

    widened(ist, 0, 0, 80)
    wt[...] = jnp.transpose(rows_of(ist, 64, 1, 80)) * INDEX_SCALE

    ipart[...] = jnp.zeros_like(ipart)

    def index_pair(jp, _):
        for e in range(2):
            iqs[jp, pl.ds(e * 128, 128), :] = rows_of(ist, 2 * jp + e, 32, 80).astype(BF16)
        d = jnp.maximum(nt(key[...], iqs[jp]), 0.0)
        w0, w1 = wt[pl.ds(2 * jp, 1), :], wt[pl.ds(2 * jp + 1, 1), :]
        ipart[...] += d[:, :128] * w0 + d[:, 128:] * w1
        return 0

    lax.fori_loop(0, IPAIRS // 2, index_pair, 0, unroll=2)
    p1.step3()
    p2.step2()
    lax.fori_loop(IPAIRS // 2, IPAIRS, index_pair, 0, unroll=2)
    hcopy = remote(ipart, irecv, hsend, hrecv, at(hd_=1 - hd))
    hcopy.start()
    p1.step4()
    widened(hst, 0, 80, 96)

    wcopy.wait()
    half = lax.broadcasted_iota(jnp.int32, (128, 128), 1) // 64

    def prepare(p, dest):
        base = (p // 16) * 6144
        pr = lax.rem(p, 16)
        rp = rows_of(hst, base + 64 + pr, 16, 96)
        for e in range(2):
            qn = rows_of(hst, base + pr * 2 + e, 32, 96).astype(BF16)
            dest[pl.ds(e * 128, 128), pl.ds(0, 512)] = nn(qn, wv[2 * p + e]).astype(BF16)
            dest[pl.ds(e * 128, 128), pl.ds(512, 128)] = jnp.where(half == e, rp, 0.0).astype(BF16)

    def scores(src, dest):
        peak = None
        for a in range(KEYS // SCH):
            t = nt(lext[pl.ds(a * SCH, SCH), :], src[...])
            dest[pl.ds(a * SCH, SCH), :] = t
            top = jnp.max(t.reshape(SCH // 8, 8, 256), axis=0)
            peak = top if peak is None else jnp.maximum(peak, top)
        return jnp.max(peak, axis=0, keepdims=True)

    def powers(p, src, peak):
        total = None
        for a in range(KEYS // SCH):
            pw = jnp.exp2((src[pl.ds(a * SCH, SCH), :] - peak) * SCORE_K)
            pm[p, pl.ds(a * SCH, SCH), :] = pw.astype(BF16)
            part = jnp.sum(pw.reshape(SCH // 8, 8, 256), axis=0)
            total = part if total is None else total + part
        l = jnp.sum(total, axis=0, keepdims=True)
        m = peak * SCORE_K
        part, gi, row = p // 16, lax.rem(p, 16) // 2, lax.rem(p, 2) * 2
        for e in range(2):
            st[part, gi, pl.ds(row + e, 1), :] = m[:, e * 128 : e * 128 + 128]
            st[part, gi, pl.ds(4 + row + e, 1), :] = l[:, e * 128 : e * 128 + 128]

    def merged(ref, part):
        mm = ref[part, 0, pl.ds(0, 4), :]
        jm = ref[part, 0, pl.ds(8, 1), :]
        for k in range(1, 8):
            mm = jnp.maximum(mm, ref[part, k, pl.ds(0, 4), :])
            jm = jnp.maximum(jm, ref[part, k, pl.ds(8, 1), :])
        ll, jl = jnp.zeros_like(mm), jnp.zeros_like(jm)
        for k in range(8):
            ll += ref[part, k, pl.ds(4, 4), :] * jnp.exp2(ref[part, k, pl.ds(0, 4), :] - mm)
            jl += ref[part, k, pl.ds(9, 1), :] * jnp.exp2(ref[part, k, pl.ds(8, 1), :] - jm)
        return mm, ll, jm, jl

    def put(ref, part, values):
        for at_row, rows, v in zip((0, 4, 8, 9), (4, 4, 1, 1), values):
            ref[part, pl.ds(at_row, rows), :] = v

    def begin(copies):
        for cp in copies:
            cp.start()

    def finish(copies):
        for cp in copies:
            cp.wait()

    def swap(copies):
        begin(copies)
        finish(copies)

    class Stats:
        def __init__(self, part):
            self.part = part
            self.c1, self.c2, self.c3 = [], [], []
            for k in range(1, 8):
                p, dev = peer1(k)
                self.c1.append(remote(st.at[part, p], r1.at[part, g1], s1send.at[part, k], s1recv.at[part, k], dev))
                self.c3.append(remote(s3.at[part], r3.at[part, g1], s3send.at[part, k], s3recv.at[part, k], dev))
                p, dev = peer2(k)
                self.c2.append(remote(s2.at[part], r2.at[part, g2], s2send.at[part, k], s2recv.at[part, k], dev))

        def step1(self):
            r1[self.part, g1] = st[self.part, g1]
            begin(self.c1)

        def step2(self):
            finish(self.c1)
            put(s2, self.part, merged(r1, self.part))
            r2[self.part, g2] = s2[self.part]
            begin(self.c2)

        def step3(self):
            finish(self.c2)
            put(s3, self.part, merged(r2, self.part))
            r3[self.part, g1] = s3[self.part]
            begin(self.c3)

        def step4(self):
            finish(self.c3)
            for gi in range(8):
                st[self.part, gi, pl.ds(0, 4), :] = jnp.exp2(
                    st[self.part, gi, pl.ds(0, 4), :] - r3[self.part, gi, pl.ds(0, 4), :]
                ) / (r3[self.part, gi, pl.ds(4, 4), :] * 128.0)

    def index_stats():
        hcopy.wait()
        it = jnp.where(seen(), (ipart[...] + irecv[...]) * LOG2E, MASKED)
        im = jnp.max(it, axis=0, keepdims=True)
        il = jnp.sum(jnp.exp2(it - im), axis=0, keepdims=True)
        mis[...] = it
        for gi in range(8):
            st[0, gi, pl.ds(8, 1), :] = im
            st[0, gi, pl.ds(9, 1), :] = il

    st[...] = jnp.zeros_like(st)
    stats0, stats1 = Stats(0), Stats(1)

    prepare(0, lq)
    peak0 = scores(lq, sc)
    prepare(1, lq2)

    def two_pairs(i, peak):
        p = 2 * i
        peak2 = scores(lq2, sc2)
        prepare(jnp.minimum(p + 2, PAIRS - 1), lq)
        powers(p, sc, peak)
        nxt = scores(lq, sc)
        prepare(jnp.minimum(p + 3, PAIRS - 1), lq2)
        powers(p + 1, sc2, peak2)

        @pl.when(i == 2)
        def _():
            p2.step3()

        @pl.when(i == 6)
        def _():
            p2.step4()
            widened(hst, 6144, 176, 96)

        @pl.when(i == 7)
        def _():
            index_stats()
            stats0.step1()

        @pl.when(i == 10)
        def _():
            stats0.step2()

        @pl.when(i == 12)
        def _():
            stats0.step3()

        @pl.when(i == 15)
        def _():
            stats0.step4()

        return nxt

    lax.fori_loop(0, PAIRS // 2, two_pairs, peak0)

    def add_heads(part, ch, acc):
        def add_group(gi, acc):
            for a in range(2):
                pw = pm[part * 16 + gi * 2 + a, pl.ds(ch * TCH, TCH), :].astype(F32)
                acc = acc + pw[:, :128] * st[part, gi, pl.ds(2 * a, 1), :]
                acc = acc + pw[:, 128:] * st[part, gi, pl.ds(2 * a + 1, 1), :]
            return acc

        return lax.fori_loop(0, 8, add_group, acc, unroll=2)

    def early(chs):
        for ch in chs:
            tpart[pl.ds(ch * TCH, TCH), :] = add_heads(0, ch, jnp.zeros((TCH, QUERIES), F32))

    stats1.step1()
    early(range(0, CHUNKS // 2))
    stats1.step2()
    early(range(CHUNKS // 2, CHUNKS))
    stats1.step3()
    gqt[...] = jnp.zeros_like(gqt)
    gwt[...] = jnp.zeros_like(gwt)
    jpeak, jtotal = s3[0, pl.ds(8, 1), :], s3[0, pl.ds(9, 1), :]
    stats1.step4()

    tcopies = []
    for ch in range(CHUNKS):
        rows = pl.ds(ch * TCH, TCH)
        tpart[rows, :] = add_heads(1, ch, tpart[rows, :])
        cp = remote(tpart.at[rows], trecv.at[rows], tsend.at[ch], trsem.at[ch], at(hd_=1 - hd))
        cp.start()
        tcopies.append(cp)

    kcopies = []
    for ch in range(CHUNKS):
        rows = pl.ds(ch * TCH, TCH)
        tcopies[ch].wait()
        predicted = jnp.exp2(mis[rows, :] - jpeak) / jtotal
        mis[rows, :] = (predicted - (tpart[rows, :] + trecv[rows, :])) * ALL_KEYS

        def slope_pair(jp, acc, rows=rows):
            iq = iqs[jp]
            mf = mis[rows, :]
            d = nt(key[rows, :], iq)
            parts = []
            for e in range(2):
                de = d[:, e * 128 : e * 128 + 128]
                gwt[pl.ds(2 * jp + e, 1), :] += jnp.sum(mf * jnp.maximum(de, 0.0), axis=0, keepdims=True)
                parts.append(jnp.where(de > 0, mf * wt[pl.ds(2 * jp + e, 1), :], 0.0).astype(BF16))
            sl = jnp.concatenate(parts, axis=1)
            gqt[jp] += nn(keyt[:, rows], sl)
            return acc + nn(sl, iq)

        gkp[rows, :] = lax.fori_loop(0, IPAIRS, slope_pair, jnp.zeros((TCH, IDIM), F32), unroll=UNR)
        cp = remote(gkp.at[rows], gkr.at[rows], ksend.at[ch], krsem.at[ch], at(hd_=1 - hd))
        cp.start()
        kcopies.append(cp)

    for j in range(IHEADS):
        tr = jnp.transpose(gqt[j // 2, :, pl.ds((j % 2) * 128, 128)])
        for r in range(2):
            rs[pl.ds(r * 32 + j, 64, stride=BR), :] = tr[r * 64 : r * 64 + 64]
    tw = jnp.transpose(gwt[...]) * INDEX_SCALE
    for r in range(16):
        rs[pl.ds(64 + r, 64, stride=BR), :] = tw[r * 64 : r * 64 + 64] if r < 2 else jnp.zeros((64, 128), F32)

    ccopy = remote(
        rs.at[pl.ds(pl.multiple_of((1 - c) * 32 * BR, BR), 32 * BR)], rcv, csend, crecv, other
    )
    ccopy.start()
    ccopy.wait()

    def add_core(o, _):
        oy, ox, oz = o // 8, lax.rem(o // 2, 4), lax.rem(o, 2)
        here = pl.ds(pl.multiple_of(o * BR, BR), BR)
        v = rcv[here, :] + rs[pl.ds(pl.multiple_of((c * 32 + o) * BR, BR), BR), :]
        rcv[here, :] = v
        w = v[64:72]
        low = w - w.astype(BF16).astype(F32)
        sb[oy, ox, oz] = jnp.concatenate([v[:72], low], axis=0).astype(BF16)
        return 0

    lax.fori_loop(0, 32, add_core, 0)
    cps = []
    for k in range(1, 4):
        yp, xp = lax.rem(y + k, 4), lax.rem(x + k, 4)
        cps.append(remote(sb.at[yp, four, 0], rya.at[k], ysend.at[k], yrecv.at[k], at(y_=yp)))
        cps.append(remote(sb.at[four, xp, 1], rxb.at[k], xsend.at[k], xrecv.at[k], at(x_=xp)))
    swap(cps)

    for o in range(4):
        for dest, src, index in (
            (0, rya, (y * 4 + o) * 2),
            (1, rxb, (o * 4 + x) * 2 + 1),
        ):
            v = rcv[pl.ds(pl.multiple_of(index * BR, BR), BR), :]
            main, w = v[:64], v[64:72]
            for k in range(1, 4):
                vk = src[k, o].astype(F32)
                main, w = main + vk[:64], w + (vk[64:72] + vk[72:])
            pab[dest, o, pl.ds(0, 64), :] = main
            pab[dest, o, pl.ds(64, 8), :] = w
            pab[dest, o, pl.ds(72, 8), :] = jnp.zeros((8, 128), F32)
    mine = x * (1 - zh) + y * zh
    theirs = x * zh + y * (1 - zh)
    rz[zh * 4 + mine] = pab[zh, mine]
    cps = []
    for k in range(1, 4):
        yp, xp = lax.rem(y + k, 4), lax.rem(x + k, 4)
        slot = zh * 4 + x
        cps.append(remote(pab.at[0, xp], rz.at[slot], zsend.at[k], zrecv.at[slot], at(zh_=0, x_=xp)))
        slot = zh * 4 + y
        cps.append(remote(pab.at[1, yp], rz.at[slot], zsend.at[3 + k], zrecv.at[slot], at(zh_=1, y_=yp)))
    slot = zh * 4 + theirs
    cps.append(remote(pab.at[1 - zh, theirs], rz.at[slot], zsend.at[0], zrecv.at[slot], across))
    begin(cps)
    for cp in cps:
        cp.wait_send()
    for k in range(1, 8):
        slot = lax.rem(zh * 4 + mine + k, 8)
        remote(pab.at[0, 0], rz.at[slot], zsend.at[0], zrecv.at[slot], across).wait_recv()
    total = rz[0]
    for k in range(1, 8):
        total = total + rz[k]
    raw[pl.ds(0, BR), :] = total
    for r in range(2):
        for j in range(IHEADS):
            gq_out[pl.ds(r, 1), pl.ds(j * 128, 128)] = raw[pl.ds(r * 32 + j, 1), :]
        gw_out[pl.ds(r, 1), :] = raw[pl.ds(64 + r, 1), pl.ds(0, IHEADS)]
    for cp in kcopies:
        cp.wait()
    gk_out[...] = gkp[...] + gkr[...]


def shards(q_heads, w_uk, latent_t, index_query, index_key, head_weight, query_pos, key_start):
    vm = pl.BlockSpec(memory_space=pltpu.VMEM)
    dma = pltpu.SemaphoreType.DMA

    def v(*shape, dtype=F32):
        return pltpu.VMEM(shape, dtype)

    return pl.pallas_call(
        body,
        out_shape=(
            jax.ShapeDtypeStruct((2, IHEADS * IDIM), F32),
            jax.ShapeDtypeStruct((KEYS, IDIM), F32),
            jax.ShapeDtypeStruct((2, IHEADS), F32),
        ),
        in_specs=[vm, vm, vm, vm, vm, pl.BlockSpec(memory_space=pl.ANY), vm, vm],
        out_specs=(vm, vm, vm),
        scratch_shapes=[
            v(272, 128),
            v(8, 128, dtype=jnp.int32),
            v(8, 128, dtype=jnp.int32),
            v(2, 4, 4, 2, 272, 128, dtype=BF16),
            v(2 * 64 * 96, 128),
            v(64 * 80, 128),
            v(HEADS, NOPE, 512, dtype=BF16),
            v(KEYS, 768, dtype=BF16),
            v(256, 768, dtype=BF16),
            v(256, 768, dtype=BF16),
            v(KEYS, 256),
            v(KEYS, 256),
            v(PAIRS, KEYS, 256, dtype=BF16),
            v(IPAIRS, 256, 128, dtype=BF16),
            v(128, 128),
            v(KEYS, 128),
            v(KEYS, 128),
            v(2, 8, 16, 128),
            v(2, 8, 16, 128),
            v(2, 16, 128),
            v(2, 8, 16, 128),
            v(2, 16, 128),
            v(2, 8, 16, 128),
            v(KEYS, 128),
            v(KEYS, 128),
            v(KEYS, 128),
            v(128, KEYS, dtype=BF16),
            v(IPAIRS, 128, 256),
            v(128, 128),
            v(KEYS, 128),
            v(KEYS, 128),
            v(64 * BR, 128),
            v(32 * BR, 128),
            v(4, 4, 2, BR, 128, dtype=BF16),
            v(4, 4, BR, 128, dtype=BF16),
            v(4, 4, BR, 128, dtype=BF16),
            v(2, 4, BR, 128),
            v(8, BR, 128),
            dma, dma((NCOPY,)), dma((NCOPY,)), dma, dma,
            dma((CHUNKS,)), dma((CHUNKS,)), dma((CHUNKS,)), dma((CHUNKS,)),
            dma((2, 8)), dma((2, 8)), dma((2, 8)), dma((2, 8)), dma((2, 8)), dma((2, 8)),
            dma, dma, dma((4,)), dma((4,)), dma((4,)), dma((4,)),
            dma((8,)), dma((8,)),
        ],
        compiler_params=pltpu.CompilerParams(
            collective_id=0, has_side_effects=True, vmem_limit_bytes=63 * 1024 * 1024
        ),
    )(
        q_heads, index_query, head_weight, key_start.reshape(1, QUERIES), query_pos.reshape(1, QUERIES),
        w_uk, latent_t, index_key,
    )


def solution(mesh):
    torus = Mesh(mesh.devices.reshape(2, 4, 4, 2, 2), AXES)
    placed = (
        P(CTX, "head"),
        P("head", None, None),
        P(None, CTX),
        P(CTX, "head"),
        P(CTX, None),
        P(CTX, "head"),
        P(),
        P(),
    )
    return jax.shard_map(
        shards,
        mesh=torus,
        in_specs=placed,
        out_specs=(P(CTX, "head"), P(CTX, None), P(CTX, "head")),
        check_vma=False,
    )
```

```python
import jax
import jax.numpy as jnp
from jax import lax
from jax.experimental import pallas as pl
from jax.experimental.pallas import tpu as pltpu
from jax.sharding import Mesh
from jax.sharding import PartitionSpec as P

NOPE = 128
ROPE = 64
IDIM = 128
CTX = ("zh", "y", "x", "c")
AXES = ("zh", "y", "x", "c", "head")
MESH_ID = pl.DeviceIdType.MESH

HEADS = 64
IHEADS = 32
QUERIES = 128
KEYS = 1024
ALL_KEYS = 65536
PAIRS = HEADS // 2
IPAIRS = IHEADS // 2
LOG2E = 1.4426950408889634
SCORE_K = (NOPE + ROPE) ** -0.5 * LOG2E
INDEX_SCALE = (IDIM * 64) ** -0.5
MASKED = -1.0e30
CUTS = ((0, 256), (256, 256), (512, 256), (768, 256))
CHUNKS = len(CUTS)
BR = 80
NCOPY = 84
UNR = 4
PUN = 4
DCH = 1024
SCH = 256

F32 = jnp.float32
BF16 = jnp.bfloat16


def nt(a, b):
    return lax.dot_general(a, b, (((1,), (1,)), ((), ())), preferred_element_type=F32)


def nn(a, b):
    return lax.dot_general(a, b, (((1,), (0,)), ((), ())), preferred_element_type=F32)


def body(
    qh, iqh, hw, start_in, pos_in, wuk, lat, key, gq_out, gk_out, gw_out,
    raw, low, high, g, hst, ist, wv, lext, rot, eyes, sc, sc2, pm, iqs, wt, ipart, irecv,
    st, r1, s2, r2, s3, r3, tpart, trecv, mis, keyt, gqt, gwt, gkp, gkr,
    rs, rcv, sb, rya, rxb, pab, rz,
    wsem, gsend, grecv, hsend, hrecv, tsend, trsem, ksend, krsem,
    s1send, s1recv, s2send, s2recv, s3send, s3recv, csend, crecv, ysend, yrecv, xsend, xrecv,
    zsend, zrecv,
):
    zh, y, x, c, hd = (lax.axis_index(a) for a in AXES)

    def at(zh_=None, y_=None, x_=None, c_=None, hd_=None):
        return (
            zh if zh_ is None else zh_, y if y_ is None else y_, x if x_ is None else x_,
            c if c_ is None else c_, hd if hd_ is None else hd_,
        )

    def remote(src, dst, ss, rsem, dev):
        return pltpu.make_async_remote_copy(
            src_ref=src, dst_ref=dst, send_sem=ss, recv_sem=rsem, device_id=dev, device_id_type=MESH_ID
        )

    g1, g2 = c * 4 + x, zh * 4 + y

    def peer1(k):
        p = lax.rem(g1 + k, 8)
        return p, at(x_=lax.rem(p, 4), c_=p // 4)

    def peer2(k):
        p = lax.rem(g2 + k, 8)
        return p, at(zh_=p // 4, y_=lax.rem(p, 4))

    barrier = pltpu.get_barrier_semaphore()
    for k in range(1, 8):
        pl.semaphore_signal(barrier, inc=1, device_id=peer1(k)[1], device_id_type=MESH_ID)
        pl.semaphore_signal(barrier, inc=1, device_id=peer2(k)[1], device_id_type=MESH_ID)
    pl.semaphore_signal(barrier, inc=1, device_id=at(hd_=1 - hd), device_id_type=MESH_ID)
    for k in range(1, 4):
        pl.semaphore_signal(
            barrier, inc=1, device_id=at(zh_=1 - zh, x_=lax.rem(x + k, 4)), device_id_type=MESH_ID
        )
    wcopy = pltpu.make_async_copy(wuk, wv, wsem)
    wcopy.start()

    lane = lax.broadcasted_iota(jnp.int32, (2, 128), 1)
    raw[pl.ds(64, 16), :] = jnp.zeros((16, 128), F32)
    for r in range(2):
        raw[pl.ds(64 + r, 1), pl.ds(0, IHEADS)] = hw[pl.ds(r, 1), :].astype(F32)
    for j in range(IHEADS):
        t = iqh[:, pl.ds(j * 128, 128)].astype(F32)
        for r in range(2):
            raw[pl.ds(r * 32 + j, 1), :] = t[r : r + 1]
    for p in range(PAIRS):
        t0, t1, t2 = (qh[:, pl.ds(p * 384 + a * 128, 128)].astype(F32) for a in range(3))
        rope = jnp.where(lane < 64, t1, t2)
        second = pltpu.roll(jnp.where(lane < 64, t2, t1), 64, 1)
        base = 80 + (p // 16) * 96
        hl, pr = (p % 16) * 2, p % 16
        for r in range(2):
            raw[pl.ds(base + r * 32 + hl, 1), :] = t0[r : r + 1]
            raw[pl.ds(base + r * 32 + hl + 1, 1), :] = second[r : r + 1]
            raw[pl.ds(base + 64 + r * 16 + pr, 1), :] = rope[r : r + 1]
    g[c, y, x, zh] = raw[...].astype(BF16)
    qa = lax.broadcasted_iota(jnp.int32, (128, 128), 0)
    qb = lax.broadcasted_iota(jnp.int32, (128, 128), 1)
    place = (
        lax.rem(qb, 2) * 64 + lax.rem(qb // 8, 4) * 16 + lax.rem(qb // 2, 4) * 4 + lax.rem(qb // 32, 2) * 2 + qb // 64
    )
    moved = (qa == place).astype(F32).astype(BF16)

    def ordered(ref):
        v = jnp.broadcast_to(ref[...], (8, 128))
        top = nn((v // 256).astype(F32).astype(BF16), moved)
        rest = nn(lax.rem(v, 256).astype(F32).astype(BF16), moved)
        return (top * 256.0 + rest).astype(jnp.int32)

    low[...] = ordered(start_in)
    high[...] = ordered(pos_in)
    pl.semaphore_wait(barrier, 18)

    number = iter(range(NCOPY))

    def gcopy(ref, dev):
        k = next(number)
        return remote(ref, ref, gsend.at[k], grecv.at[k], dev)

    xr, xl = lax.rem(x + 1, 4), lax.rem(x + 3, 4)
    yr, yl = lax.rem(y + 1, 4), lax.rem(y + 3, 4)
    xo, yo = lax.rem(x + 2, 4), lax.rem(y + 2, 4)
    both, four = pl.ds(0, 2), pl.ds(0, 4)
    other, across = at(c_=1 - c), at(zh_=1 - zh)
    near = (1, 3, 2)
    peers_zx = [at(x_=lax.rem(x + k, 4)) for k in near] + [across]
    peers_zx += [at(zh_=1 - zh, x_=lax.rem(x + k, 4)) for k in near]
    peers_zy = [at(y_=lax.rem(y + k, 4)) for k in near] + [across]
    peers_zy += [at(zh_=1 - zh, y_=lax.rem(y + k, 4)) for k in near]

    class Piece:
        def __init__(self, row, na, nb):
            ra, rb = pl.ds(row, na), pl.ds(row + na, nb)
            own_a, own_b = g.at[c, y, x, zh, ra], g.at[c, y, x, zh, rb]
            self.a1 = [gcopy(own_a, d) for d in peers_zx]
            self.b1 = [gcopy(own_b, d) for d in peers_zy]
            self.a2 = [gcopy(g.at[c, y, four, both, ra], at(y_=q)) for q in (yr, yl, yo)]
            self.b2 = [gcopy(g.at[c, four, x, both, rb], at(x_=q)) for q in (xr, xl, xo)]
            self.ca = [gcopy(g.at[c, q, four, both, ra], other) for q in (y, yl, yr, yo)]
            self.cb = [gcopy(g.at[c, four, q, both, rb], other) for q in (x, xl, xr, xo)]

        def step1(self):
            for cp in self.a1 + self.b1:
                cp.start()

        def step2(self):
            for before, after, core in ((self.a1, self.a2, self.ca), (self.b1, self.b2, self.cb)):
                for cp in before:
                    cp.wait_recv()
                for cp in after:
                    cp.start()
                core[0].start()

        def step3(self):
            for k in range(3):
                for before, core in ((self.a2, self.ca), (self.b2, self.cb)):
                    before[k].wait_recv()
                    core[1 + k].start()

        def step4(self):
            for cp in self.ca + self.cb:
                cp.wait()
            for cp in self.a1 + self.b1 + self.a2 + self.b2:
                cp.wait_send()

    first = (((zh * 4 + y) * 4 + x) * 2 + c) * KEYS

    def seen():
        ids = first + lax.broadcasted_iota(jnp.int32, (KEYS, QUERIES), 0)
        return (ids >= low[pl.ds(0, 1), :]) & (ids <= high[pl.ds(0, 1), :])

    def turn(a):
        lext[:, pl.ds(a * 128, 128)] = jnp.transpose(lat[pl.ds(a * 128, 128), :].astype(F32)).astype(BF16)

    p0, p1, p2 = Piece(0, 32, 48), Piece(80, 48, 48), Piece(176, 48, 48)
    p0.step1()
    p1.step1()
    lext[:, pl.ds(640, 128)] = jnp.where(seen(), 0.0, MASKED).astype(BF16)
    eye = (qa == qb).astype(F32).astype(BF16)
    eyes[pl.ds(0, 128), :] = eye
    eyes[pl.ds(128, 128), :] = eye
    turn(0)
    p0.step2()
    p2.step1()
    turn(1)
    turn(2)
    turn(3)
    p1.step2()
    rope_rows = lat[pl.ds(512, 64), :].astype(F32)
    lext[:, pl.ds(512, 128)] = jnp.transpose(jnp.concatenate([rope_rows, rope_rows], axis=0)).astype(BF16)
    keyt[...] = jnp.transpose(key[...].astype(F32)).astype(BF16)
    p0.step3()
    p0.step4()

    def widened(dest, base, row, rows):
        def one(o, _):
            oc, oy, ox, oz = o // 32, lax.rem(o // 8, 4), lax.rem(o // 2, 4), lax.rem(o, 2)
            dest[pl.ds(pl.multiple_of(base + o * rows, 16), rows), :] = g[oc, oy, ox, oz, pl.ds(row, rows), :].astype(F32)
            return 0

        lax.fori_loop(0, 64, one, 0)

    def rows_of(ref, offset, step, stride):
        return jnp.concatenate(
            [ref[pl.ds(offset + r * step, 64, stride=stride), :] for r in range(2)], axis=0
        )

    widened(ist, 0, 0, 80)
    wt[...] = jnp.transpose(rows_of(ist, 64, 1, 80)) * INDEX_SCALE

    ipart[...] = jnp.zeros_like(ipart)

    def index_pair(jp, _):
        for e in range(2):
            iqs[jp, pl.ds(e * 128, 128), :] = rows_of(ist, 2 * jp + e, 32, 80).astype(BF16)
        d = jnp.maximum(nt(key[...], iqs[jp]), 0.0)
        w0, w1 = wt[pl.ds(2 * jp, 1), :], wt[pl.ds(2 * jp + 1, 1), :]
        ipart[...] += d[:, :128] * w0 + d[:, 128:] * w1
        return 0

    lax.fori_loop(0, IPAIRS // 2, index_pair, 0, unroll=2)
    p1.step3()
    p2.step2()
    lax.fori_loop(IPAIRS // 2, IPAIRS, index_pair, 0, unroll=2)
    hcopy = remote(ipart, irecv, hsend, hrecv, at(hd_=1 - hd))
    hcopy.start()
    p1.step4()
    widened(hst, 0, 80, 96)

    wcopy.wait()
    half = lax.broadcasted_iota(jnp.int32, (128, 128), 1) // 64

    def prepare(p, _):
        base = (p // 16) * 6144
        pr = lax.rem(p, 16)
        rp = rows_of(hst, base + 64 + pr, 16, 96)
        for e in range(2):
            qn = rows_of(hst, base + pr * 2 + e, 32, 96).astype(BF16)
            wv[2 * p + e] = nn(qn, wv[2 * p + e]).astype(BF16)
            rot[p, pl.ds(e * 128, 128), :] = jnp.where(half == e, rp, 0.0).astype(BF16)
        return 0

    def scores(f, dest):
        pairs = [
            jnp.concatenate(
                [jnp.concatenate([wv[2 * p], wv[2 * p + 1]], axis=0), rot[p], eyes[...]], axis=1
            )
            for p in (2 * f, 2 * f + 1)
        ]
        query = jnp.concatenate(pairs, axis=0)
        peak = None
        for a in range(KEYS // DCH):
            t = nt(lext[pl.ds(a * DCH, DCH), :], query)
            dest[pl.ds(a * DCH, DCH), :] = t
            top = jnp.max(t.reshape(DCH // 8, 8, 512), axis=0)
            peak = top if peak is None else jnp.maximum(peak, top)
        return jnp.max(peak, axis=0, keepdims=True)

    def powers(f, src, peaks):
        for e in range(2):
            powers_of(2 * f + e, src, pl.ds(e * 256, 256), peaks[:, e * 256 : e * 256 + 256])

    def powers_of(p, src, cols, peak):
        total = None
        for a in range(KEYS // SCH):
            pw = jnp.exp2((src[pl.ds(a * SCH, SCH), cols] - peak) * SCORE_K)
            pm[p, pl.ds(a * SCH, SCH), :] = pw.astype(BF16)
            part = jnp.sum(pw.reshape(SCH // 8, 8, 256), axis=0)
            total = part if total is None else total + part
        l = jnp.sum(total, axis=0, keepdims=True)
        m = peak * SCORE_K
        part, gi, row = p // 16, lax.rem(p, 16) // 2, lax.rem(p, 2) * 2
        for e in range(2):
            st[part, gi, pl.ds(row + e, 1), :] = m[:, e * 128 : e * 128 + 128]
            st[part, gi, pl.ds(4 + row + e, 1), :] = l[:, e * 128 : e * 128 + 128]

    def merged(ref, part):
        mm = ref[part, 0, pl.ds(0, 4), :]
        jm = ref[part, 0, pl.ds(8, 1), :]
        for k in range(1, 8):
            mm = jnp.maximum(mm, ref[part, k, pl.ds(0, 4), :])
            jm = jnp.maximum(jm, ref[part, k, pl.ds(8, 1), :])
        ll, jl = jnp.zeros_like(mm), jnp.zeros_like(jm)
        for k in range(8):
            ll += ref[part, k, pl.ds(4, 4), :] * jnp.exp2(ref[part, k, pl.ds(0, 4), :] - mm)
            jl += ref[part, k, pl.ds(9, 1), :] * jnp.exp2(ref[part, k, pl.ds(8, 1), :] - jm)
        return mm, ll, jm, jl

    def put(ref, part, values):
        for at_row, rows, v in zip((0, 4, 8, 9), (4, 4, 1, 1), values):
            ref[part, pl.ds(at_row, rows), :] = v

    def begin(copies):
        for cp in copies:
            cp.start()

    def finish(copies):
        for cp in copies:
            cp.wait()

    def swap(copies):
        begin(copies)
        finish(copies)

    class Stats:
        def __init__(self, part):
            self.part = part
            self.c1, self.c2, self.c3 = [], [], []
            for k in range(1, 8):
                p, dev = peer1(k)
                self.c1.append(remote(st.at[part, p], r1.at[part, g1], s1send.at[part, k], s1recv.at[part, k], dev))
                self.c3.append(remote(s3.at[part], r3.at[part, g1], s3send.at[part, k], s3recv.at[part, k], dev))
                p, dev = peer2(k)
                self.c2.append(remote(s2.at[part], r2.at[part, g2], s2send.at[part, k], s2recv.at[part, k], dev))

        def step1(self):
            r1[self.part, g1] = st[self.part, g1]
            begin(self.c1)

        def step2(self):
            finish(self.c1)
            put(s2, self.part, merged(r1, self.part))
            r2[self.part, g2] = s2[self.part]
            begin(self.c2)

        def step3(self):
            finish(self.c2)
            put(s3, self.part, merged(r2, self.part))
            r3[self.part, g1] = s3[self.part]
            begin(self.c3)

        def step4(self):
            finish(self.c3)
            for gi in range(8):
                st[self.part, gi, pl.ds(0, 4), :] = jnp.exp2(
                    st[self.part, gi, pl.ds(0, 4), :] - r3[self.part, gi, pl.ds(0, 4), :]
                ) / (r3[self.part, gi, pl.ds(4, 4), :] * 128.0)

    def index_stats():
        hcopy.wait()
        it = jnp.where(seen(), (ipart[...] + irecv[...]) * LOG2E, MASKED)
        im = jnp.max(it, axis=0, keepdims=True)
        il = jnp.sum(jnp.exp2(it - im), axis=0, keepdims=True)
        mis[...] = it
        for gi in range(8):
            st[0, gi, pl.ds(8, 1), :] = im
            st[0, gi, pl.ds(9, 1), :] = il

    st[...] = jnp.zeros_like(st)
    stats0, stats1 = Stats(0), Stats(1)

    lax.fori_loop(0, PAIRS // 2, prepare, 0, unroll=PUN)
    peak0 = scores(0, sc)

    def four_pairs(i, peak):
        peak2 = scores(2 * i + 1, sc2)
        powers(2 * i, sc, peak)
        nxt = scores(jnp.minimum(2 * i + 2, PAIRS // 2 - 1), sc)
        powers(2 * i + 1, sc2, peak2)

        @pl.when(i == 0)
        def _():
            p2.step3()

        @pl.when(i == 2)
        def _():
            p2.step4()
            widened(hst, 6144, 176, 96)
            lax.fori_loop(PAIRS // 2, PAIRS, prepare, 0, unroll=PUN)

        @pl.when(i == 3)
        def _():
            index_stats()
            stats0.step1()

        @pl.when(i == 4)
        def _():
            stats0.step2()

        @pl.when(i == 5)
        def _():
            stats0.step3()

        @pl.when(i == 7)
        def _():
            stats0.step4()

        return nxt

    lax.fori_loop(0, PAIRS // 4, four_pairs, peak0)

    def add_heads(part, ch, acc):
        def add_group(gi, acc):
            for a in range(2):
                pw = pm[part * 16 + gi * 2 + a, pl.ds(*CUTS[ch]), :].astype(F32)
                acc = acc + pw[:, :128] * st[part, gi, pl.ds(2 * a, 1), :]
                acc = acc + pw[:, 128:] * st[part, gi, pl.ds(2 * a + 1, 1), :]
            return acc

        return lax.fori_loop(0, 8, add_group, acc, unroll=2)

    def early(chs):
        for ch in chs:
            tpart[pl.ds(*CUTS[ch]), :] = add_heads(0, ch, jnp.zeros((CUTS[ch][1], QUERIES), F32))

    stats1.step1()
    early(range(0, 2))
    stats1.step2()
    early(range(2, CHUNKS))
    stats1.step3()
    gqt[...] = jnp.zeros_like(gqt)
    gwt[...] = jnp.zeros_like(gwt)
    jpeak, jtotal = s3[0, pl.ds(8, 1), :], s3[0, pl.ds(9, 1), :]
    stats1.step4()

    tcopies = []
    for ch in range(CHUNKS):
        rows = pl.ds(*CUTS[ch])
        tpart[rows, :] = add_heads(1, ch, tpart[rows, :])
        cp = remote(tpart.at[rows], trecv.at[rows], tsend.at[ch], trsem.at[ch], at(hd_=1 - hd))
        cp.start()
        tcopies.append(cp)

    kcopies = []
    for ch in range(CHUNKS):
        rows = pl.ds(*CUTS[ch])
        tcopies[ch].wait()
        predicted = jnp.exp2(mis[rows, :] - jpeak) / jtotal
        mis[rows, :] = (predicted - (tpart[rows, :] + trecv[rows, :])) * ALL_KEYS

        def slope_pair(jp, acc, rows=rows):
            iq = iqs[jp]
            mf = mis[rows, :]
            d = nt(key[rows, :], iq)
            parts = []
            for e in range(2):
                de = d[:, e * 128 : e * 128 + 128]
                gwt[pl.ds(2 * jp + e, 1), :] += jnp.sum(mf * jnp.maximum(de, 0.0), axis=0, keepdims=True)
                parts.append(jnp.where(de > 0, mf * wt[pl.ds(2 * jp + e, 1), :], 0.0).astype(BF16))
            sl = jnp.concatenate(parts, axis=1)
            gqt[jp] += nn(keyt[:, rows], sl)
            return acc + nn(sl, iq)

        gkp[rows, :] = lax.fori_loop(0, IPAIRS, slope_pair, jnp.zeros((CUTS[ch][1], IDIM), F32), unroll=UNR)
        cp = remote(gkp.at[rows], gkr.at[rows], ksend.at[ch], krsem.at[ch], at(hd_=1 - hd))
        cp.start()
        kcopies.append(cp)

    for j in range(IHEADS):
        tr = jnp.transpose(gqt[j // 2, :, pl.ds((j % 2) * 128, 128)])
        for r in range(2):
            rs[pl.ds(r * 32 + j, 64, stride=BR), :] = tr[r * 64 : r * 64 + 64]
    tw = jnp.transpose(gwt[...]) * INDEX_SCALE
    for r in range(16):
        rs[pl.ds(64 + r, 64, stride=BR), :] = tw[r * 64 : r * 64 + 64] if r < 2 else jnp.zeros((64, 128), F32)

    ccopy = remote(
        rs.at[pl.ds(pl.multiple_of((1 - c) * 32 * BR, BR), 32 * BR)], rcv, csend, crecv, other
    )
    ccopy.start()
    ccopy.wait()

    def add_core(o, _):
        oy, ox, oz = o // 8, lax.rem(o // 2, 4), lax.rem(o, 2)
        here = pl.ds(pl.multiple_of(o * BR, BR), BR)
        v = rcv[here, :] + rs[pl.ds(pl.multiple_of((c * 32 + o) * BR, BR), BR), :]
        rcv[here, :] = v
        w = v[64:72]
        low = w - w.astype(BF16).astype(F32)
        sb[oy, ox, oz] = jnp.concatenate([v[:72], low], axis=0).astype(BF16)
        return 0

    lax.fori_loop(0, 32, add_core, 0)
    cps = []
    for k in range(1, 4):
        yp, xp = lax.rem(y + k, 4), lax.rem(x + k, 4)
        cps.append(remote(sb.at[yp, four, 0], rya.at[k], ysend.at[k], yrecv.at[k], at(y_=yp)))
        cps.append(remote(sb.at[four, xp, 1], rxb.at[k], xsend.at[k], xrecv.at[k], at(x_=xp)))
    swap(cps)

    for o in range(4):
        for dest, src, index in (
            (0, rya, (y * 4 + o) * 2),
            (1, rxb, (o * 4 + x) * 2 + 1),
        ):
            v = rcv[pl.ds(pl.multiple_of(index * BR, BR), BR), :]
            main, w = v[:64], v[64:72]
            for k in range(1, 4):
                vk = src[k, o].astype(F32)
                main, w = main + vk[:64], w + (vk[64:72] + vk[72:])
            pab[dest, o, pl.ds(0, 64), :] = main
            pab[dest, o, pl.ds(64, 8), :] = w
            pab[dest, o, pl.ds(72, 8), :] = jnp.zeros((8, 128), F32)
    mine = x * (1 - zh) + y * zh
    theirs = x * zh + y * (1 - zh)
    rz[zh * 4 + mine] = pab[zh, mine]
    cps = []
    for k in range(1, 4):
        yp, xp = lax.rem(y + k, 4), lax.rem(x + k, 4)
        slot = zh * 4 + x
        cps.append(remote(pab.at[0, xp], rz.at[slot], zsend.at[k], zrecv.at[slot], at(zh_=0, x_=xp)))
        slot = zh * 4 + y
        cps.append(remote(pab.at[1, yp], rz.at[slot], zsend.at[3 + k], zrecv.at[slot], at(zh_=1, y_=yp)))
    slot = zh * 4 + theirs
    cps.append(remote(pab.at[1 - zh, theirs], rz.at[slot], zsend.at[0], zrecv.at[slot], across))
    begin(cps)
    for cp in cps:
        cp.wait_send()
    for k in range(1, 8):
        slot = lax.rem(zh * 4 + mine + k, 8)
        remote(pab.at[0, 0], rz.at[slot], zsend.at[0], zrecv.at[slot], across).wait_recv()
    total = rz[0]
    for k in range(1, 8):
        total = total + rz[k]
    raw[pl.ds(0, BR), :] = total
    for r in range(2):
        for j in range(IHEADS):
            gq_out[pl.ds(r, 1), pl.ds(j * 128, 128)] = raw[pl.ds(r * 32 + j, 1), :]
        gw_out[pl.ds(r, 1), :] = raw[pl.ds(64 + r, 1), pl.ds(0, IHEADS)]
    for cp in kcopies:
        cp.wait()
    gk_out[...] = gkp[...] + gkr[...]


def handed_on(*refs):
    count = len(refs) // 2
    for k in range(count):
        refs[count + k][...] = refs[k][...]


def shards(q_heads, w_uk, latent_t, index_query, index_key, head_weight, query_pos, key_start):
    vm = pl.BlockSpec(memory_space=pltpu.VMEM)
    dma = pltpu.SemaphoreType.DMA

    def v(*shape, dtype=F32):
        return pltpu.VMEM(shape, dtype)

    results = pl.pallas_call(
        body,
        out_shape=(
            jax.ShapeDtypeStruct((2, IHEADS * IDIM), F32),
            jax.ShapeDtypeStruct((KEYS, IDIM), F32),
            jax.ShapeDtypeStruct((2, IHEADS), F32),
        ),
        in_specs=[vm, vm, vm, vm, vm, pl.BlockSpec(memory_space=pl.ANY), vm, vm],
        out_specs=(vm, vm, vm),
        scratch_shapes=[
            v(272, 128),
            v(8, 128, dtype=jnp.int32),
            v(8, 128, dtype=jnp.int32),
            v(2, 4, 4, 2, 272, 128, dtype=BF16),
            v(2 * 64 * 96, 128),
            v(64 * 80, 128),
            v(HEADS, NOPE, 512, dtype=BF16),
            v(KEYS, 768, dtype=BF16),
            v(PAIRS, 256, 128, dtype=BF16),
            v(256, 128, dtype=BF16),
            v(KEYS, 512),
            v(KEYS, 512),
            v(PAIRS, KEYS, 256, dtype=BF16),
            v(IPAIRS, 256, 128, dtype=BF16),
            v(128, 128),
            v(KEYS, 128),
            v(KEYS, 128),
            v(2, 8, 16, 128),
            v(2, 8, 16, 128),
            v(2, 16, 128),
            v(2, 8, 16, 128),
            v(2, 16, 128),
            v(2, 8, 16, 128),
            v(KEYS, 128),
            v(KEYS, 128),
            v(KEYS, 128),
            v(128, KEYS, dtype=BF16),
            v(IPAIRS, 128, 256),
            v(128, 128),
            v(KEYS, 128),
            v(KEYS, 128),
            v(64 * BR, 128),
            v(32 * BR, 128),
            v(4, 4, 2, BR, 128, dtype=BF16),
            v(4, 4, BR, 128, dtype=BF16),
            v(4, 4, BR, 128, dtype=BF16),
            v(2, 4, BR, 128),
            v(8, BR, 128),
            dma, dma((NCOPY,)), dma((NCOPY,)), dma, dma,
            dma((CHUNKS,)), dma((CHUNKS,)), dma((CHUNKS,)), dma((CHUNKS,)),
            dma((2, 8)), dma((2, 8)), dma((2, 8)), dma((2, 8)), dma((2, 8)), dma((2, 8)),
            dma, dma, dma((4,)), dma((4,)), dma((4,)), dma((4,)),
            dma((8,)), dma((8,)),
        ],
        compiler_params=pltpu.CompilerParams(
            collective_id=0, has_side_effects=True, vmem_limit_bytes=63 * 1024 * 1024
        ),
    )(
        q_heads, index_query, head_weight, key_start.reshape(1, QUERIES), query_pos.reshape(1, QUERIES),
        w_uk, latent_t, index_key,
    )
    return pl.pallas_call(
        handed_on,
        out_shape=tuple(jax.ShapeDtypeStruct(v.shape, v.dtype) for v in results),
        in_specs=[vm] * 3,
        out_specs=(vm,) * 3,
    )(*results)


def solution(mesh):
    torus = Mesh(mesh.devices.reshape(2, 4, 4, 2, 2), AXES)
    placed = (
        P(CTX, "head"),
        P("head", None, None),
        P(None, CTX),
        P(CTX, "head"),
        P(CTX, None),
        P(CTX, "head"),
        P(),
        P(),
    )
    return jax.shard_map(
        shards,
        mesh=torus,
        in_specs=placed,
        out_specs=(P(CTX, "head"), P(CTX, None), P(CTX, "head")),
        check_vma=False,
    )
```

```python
import jax
import jax.numpy as jnp
from jax import lax
from jax.experimental import pallas as pl
from jax.experimental.pallas import tpu as pltpu
from jax.sharding import Mesh
from jax.sharding import PartitionSpec as P

NOPE = 128
ROPE = 64
IDIM = 128
CTX = ("zh", "y", "x", "c")
AXES = ("zh", "y", "x", "c", "head")
MESH_ID = pl.DeviceIdType.MESH

HEADS = 64
IHEADS = 32
QUERIES = 128
KEYS = 1024
ALL_KEYS = 65536
PAIRS = HEADS // 2
IPAIRS = IHEADS // 2
LOG2E = 1.4426950408889634
SCORE_K = (NOPE + ROPE) ** -0.5 * LOG2E
INDEX_SCALE = (IDIM * 64) ** -0.5
MASKED = -1.0e30
CUTS = ((0, 256), (256, 256), (512, 512))
CHUNKS = len(CUTS)
BR = 80
NCOPY = 84
UNR = 8
PUN = 8
DCH = 1024
SCH = 256

F32 = jnp.float32
BF16 = jnp.bfloat16


def nt(a, b):
    return lax.dot_general(a, b, (((1,), (1,)), ((), ())), preferred_element_type=F32)


def nn(a, b):
    return lax.dot_general(a, b, (((1,), (0,)), ((), ())), preferred_element_type=F32)


def body(
    qh, iqh, hw, start_in, pos_in, wuk, lat, key, gq_out, gk_out, gw_out,
    raw, low, high, g, hst, ist, wv, lext, rot, eyes, sc, sc2, pm, iqs, wt, ipart, irecv,
    st, r1, s2, r2, s3, r3, tpart, trecv, mis, keyt, gqt, gwt, gkp, gkr,
    rs, rcv, sb, rya, rxb, pab, rz,
    wsem, gsend, grecv, hsend, hrecv, tsend, trsem, ksend, krsem,
    s1send, s1recv, s2send, s2recv, s3send, s3recv, csend, crecv, ysend, yrecv, xsend, xrecv,
    zsend, zrecv,
):
    zh, y, x, c, hd = (lax.axis_index(a) for a in AXES)

    def at(zh_=None, y_=None, x_=None, c_=None, hd_=None):
        return (
            zh if zh_ is None else zh_, y if y_ is None else y_, x if x_ is None else x_,
            c if c_ is None else c_, hd if hd_ is None else hd_,
        )

    def remote(src, dst, ss, rsem, dev):
        return pltpu.make_async_remote_copy(
            src_ref=src, dst_ref=dst, send_sem=ss, recv_sem=rsem, device_id=dev, device_id_type=MESH_ID
        )

    g1, g2 = c * 4 + x, zh * 4 + y

    def peer1(k):
        p = lax.rem(g1 + k, 8)
        return p, at(x_=lax.rem(p, 4), c_=p // 4)

    def peer2(k):
        p = lax.rem(g2 + k, 8)
        return p, at(zh_=p // 4, y_=lax.rem(p, 4))

    barrier = pltpu.get_barrier_semaphore()
    for k in range(1, 8):
        pl.semaphore_signal(barrier, inc=1, device_id=peer1(k)[1], device_id_type=MESH_ID)
        pl.semaphore_signal(barrier, inc=1, device_id=peer2(k)[1], device_id_type=MESH_ID)
    pl.semaphore_signal(barrier, inc=1, device_id=at(hd_=1 - hd), device_id_type=MESH_ID)
    for k in range(1, 4):
        pl.semaphore_signal(
            barrier, inc=1, device_id=at(zh_=1 - zh, x_=lax.rem(x + k, 4)), device_id_type=MESH_ID
        )
    wcopy = pltpu.make_async_copy(wuk, wv, wsem)
    wcopy.start()

    lane = lax.broadcasted_iota(jnp.int32, (2, 128), 1)
    raw[pl.ds(64, 16), :] = jnp.zeros((16, 128), F32)
    for r in range(2):
        raw[pl.ds(64 + r, 1), pl.ds(0, IHEADS)] = hw[pl.ds(r, 1), :].astype(F32)
    for j in range(IHEADS):
        t = iqh[:, pl.ds(j * 128, 128)].astype(F32)
        for r in range(2):
            raw[pl.ds(r * 32 + j, 1), :] = t[r : r + 1]
    for p in range(PAIRS):
        t0, t1, t2 = (qh[:, pl.ds(p * 384 + a * 128, 128)].astype(F32) for a in range(3))
        rope = jnp.where(lane < 64, t1, t2)
        second = pltpu.roll(jnp.where(lane < 64, t2, t1), 64, 1)
        base = 80 + (p // 16) * 96
        hl, pr = (p % 16) * 2, p % 16
        for r in range(2):
            raw[pl.ds(base + r * 32 + hl, 1), :] = t0[r : r + 1]
            raw[pl.ds(base + r * 32 + hl + 1, 1), :] = second[r : r + 1]
            raw[pl.ds(base + 64 + r * 16 + pr, 1), :] = rope[r : r + 1]
    g[c, y, x, zh] = raw[...].astype(BF16)
    qa = lax.broadcasted_iota(jnp.int32, (128, 128), 0)
    qb = lax.broadcasted_iota(jnp.int32, (128, 128), 1)
    place = (
        lax.rem(qb, 2) * 64 + lax.rem(qb // 8, 4) * 16 + lax.rem(qb // 2, 4) * 4 + lax.rem(qb // 32, 2) * 2 + qb // 64
    )
    moved = (qa == place).astype(F32).astype(BF16)

    def ordered(ref):
        v = jnp.broadcast_to(ref[...], (8, 128))
        top = nn((v // 256).astype(F32).astype(BF16), moved)
        rest = nn(lax.rem(v, 256).astype(F32).astype(BF16), moved)
        return (top * 256.0 + rest).astype(jnp.int32)

    low[...] = ordered(start_in)
    high[...] = ordered(pos_in)
    pl.semaphore_wait(barrier, 18)

    number = iter(range(NCOPY))

    def gcopy(ref, dev):
        k = next(number)
        return remote(ref, ref, gsend.at[k], grecv.at[k], dev)

    xr, xl = lax.rem(x + 1, 4), lax.rem(x + 3, 4)
    yr, yl = lax.rem(y + 1, 4), lax.rem(y + 3, 4)
    xo, yo = lax.rem(x + 2, 4), lax.rem(y + 2, 4)
    both, four = pl.ds(0, 2), pl.ds(0, 4)
    other, across = at(c_=1 - c), at(zh_=1 - zh)
    near = (1, 3, 2)
    peers_zx = [at(x_=lax.rem(x + k, 4)) for k in near] + [across]
    peers_zx += [at(zh_=1 - zh, x_=lax.rem(x + k, 4)) for k in near]
    peers_zy = [at(y_=lax.rem(y + k, 4)) for k in near] + [across]
    peers_zy += [at(zh_=1 - zh, y_=lax.rem(y + k, 4)) for k in near]

    class Piece:
        def __init__(self, row, na, nb):
            ra, rb = pl.ds(row, na), pl.ds(row + na, nb)
            own_a, own_b = g.at[c, y, x, zh, ra], g.at[c, y, x, zh, rb]
            self.a1 = [gcopy(own_a, d) for d in peers_zx]
            self.b1 = [gcopy(own_b, d) for d in peers_zy]
            self.a2 = [gcopy(g.at[c, y, four, both, ra], at(y_=q)) for q in (yr, yl, yo)]
            self.b2 = [gcopy(g.at[c, four, x, both, rb], at(x_=q)) for q in (xr, xl, xo)]
            self.ca = [gcopy(g.at[c, q, four, both, ra], other) for q in (y, yl, yr, yo)]
            self.cb = [gcopy(g.at[c, four, q, both, rb], other) for q in (x, xl, xr, xo)]

        def step1(self):
            for cp in self.a1 + self.b1:
                cp.start()

        def step2(self):
            for before, after, core in ((self.a1, self.a2, self.ca), (self.b1, self.b2, self.cb)):
                for cp in before:
                    cp.wait_recv()
                for cp in after:
                    cp.start()
                core[0].start()

        def step3(self):
            for k in range(3):
                for before, core in ((self.a2, self.ca), (self.b2, self.cb)):
                    before[k].wait_recv()
                    core[1 + k].start()

        def step4(self):
            for cp in self.ca + self.cb:
                cp.wait()
            for cp in self.a1 + self.b1 + self.a2 + self.b2:
                cp.wait_send()

    first = (((zh * 4 + y) * 4 + x) * 2 + c) * KEYS

    def seen():
        ids = first + lax.broadcasted_iota(jnp.int32, (KEYS, QUERIES), 0)
        return (ids >= low[pl.ds(0, 1), :]) & (ids <= high[pl.ds(0, 1), :])

    def turn(a):
        lext[:, pl.ds(a * 128, 128)] = jnp.transpose(lat[pl.ds(a * 128, 128), :].astype(F32)).astype(BF16)

    p0, p1, p2 = Piece(0, 32, 48), Piece(80, 48, 48), Piece(176, 48, 48)
    p0.step1()
    p1.step1()
    lext[:, pl.ds(640, 128)] = jnp.where(seen(), 0.0, MASKED).astype(BF16)
    eye = (qa == qb).astype(F32).astype(BF16)
    eyes[pl.ds(0, 128), :] = eye
    eyes[pl.ds(128, 128), :] = eye
    turn(0)
    p0.step2()
    p2.step1()
    turn(1)
    turn(2)
    turn(3)
    p1.step2()
    rope_rows = lat[pl.ds(512, 64), :].astype(F32)
    lext[:, pl.ds(512, 128)] = jnp.transpose(jnp.concatenate([rope_rows, rope_rows], axis=0)).astype(BF16)
    keyt[...] = jnp.transpose(key[...].astype(F32)).astype(BF16)
    p0.step3()
    p0.step4()

    def widened(dest, base, row, rows):
        def one(o, _):
            oc, oy, ox, oz = o // 32, lax.rem(o // 8, 4), lax.rem(o // 2, 4), lax.rem(o, 2)
            dest[pl.ds(pl.multiple_of(base + o * rows, 16), rows), :] = g[oc, oy, ox, oz, pl.ds(row, rows), :].astype(F32)
            return 0

        lax.fori_loop(0, 64, one, 0)

    def rows_of(ref, offset, step, stride):
        return jnp.concatenate(
            [ref[pl.ds(offset + r * step, 64, stride=stride), :] for r in range(2)], axis=0
        )

    widened(ist, 0, 0, 80)
    wt[...] = jnp.transpose(rows_of(ist, 64, 1, 80)) * INDEX_SCALE

    ipart[...] = jnp.zeros_like(ipart)

    def index_pair(jp, _):
        for e in range(2):
            iqs[jp, pl.ds(e * 128, 128), :] = rows_of(ist, 2 * jp + e, 32, 80).astype(BF16)
        d = jnp.maximum(nt(key[...], iqs[jp]), 0.0)
        w0, w1 = wt[pl.ds(2 * jp, 1), :], wt[pl.ds(2 * jp + 1, 1), :]
        ipart[...] += d[:, :128] * w0 + d[:, 128:] * w1
        return 0

    lax.fori_loop(0, IPAIRS // 2, index_pair, 0, unroll=4)
    p1.step3()
    p2.step2()
    lax.fori_loop(IPAIRS // 2, IPAIRS, index_pair, 0, unroll=4)
    hcopy = remote(ipart, irecv, hsend, hrecv, at(hd_=1 - hd))
    hcopy.start()
    p1.step4()
    widened(hst, 0, 80, 96)

    wcopy.wait()
    half = lax.broadcasted_iota(jnp.int32, (128, 128), 1) // 64

    def prepare(p, _):
        base = (p // 16) * 6144
        pr = lax.rem(p, 16)
        rp = rows_of(hst, base + 64 + pr, 16, 96)
        for e in range(2):
            qn = rows_of(hst, base + pr * 2 + e, 32, 96).astype(BF16)
            wv[2 * p + e] = nn(qn, wv[2 * p + e]).astype(BF16)
            rot[p, pl.ds(e * 128, 128), :] = jnp.where(half == e, rp, 0.0).astype(BF16)
        return 0

    def scores(f, dest):
        pairs = [
            jnp.concatenate(
                [jnp.concatenate([wv[2 * p], wv[2 * p + 1]], axis=0), rot[p], eyes[...]], axis=1
            )
            for p in (2 * f, 2 * f + 1)
        ]
        query = jnp.concatenate(pairs, axis=0)
        peak = None
        for a in range(KEYS // DCH):
            t = nt(lext[pl.ds(a * DCH, DCH), :], query)
            dest[pl.ds(a * DCH, DCH), :] = t
            top = jnp.max(t.reshape(DCH // 8, 8, 512), axis=0)
            peak = top if peak is None else jnp.maximum(peak, top)
        return jnp.max(peak, axis=0, keepdims=True)

    def powers(f, src, peaks):
        for e in range(2):
            powers_of(2 * f + e, src, pl.ds(e * 256, 256), peaks[:, e * 256 : e * 256 + 256])

    def powers_of(p, src, cols, peak):
        total = None
        for a in range(KEYS // SCH):
            pw = jnp.exp2((src[pl.ds(a * SCH, SCH), cols] - peak) * SCORE_K)
            pm[p, pl.ds(a * SCH, SCH), :] = pw.astype(BF16)
            part = jnp.sum(pw.reshape(SCH // 8, 8, 256), axis=0)
            total = part if total is None else total + part
        l = jnp.sum(total, axis=0, keepdims=True)
        m = peak * SCORE_K
        part, gi, row = p // 16, lax.rem(p, 16) // 2, lax.rem(p, 2) * 2
        for e in range(2):
            st[part, gi, pl.ds(row + e, 1), :] = m[:, e * 128 : e * 128 + 128]
            st[part, gi, pl.ds(4 + row + e, 1), :] = l[:, e * 128 : e * 128 + 128]

    def merged(ref, part):
        mm = ref[part, 0, pl.ds(0, 4), :]
        jm = ref[part, 0, pl.ds(8, 1), :]
        for k in range(1, 8):
            mm = jnp.maximum(mm, ref[part, k, pl.ds(0, 4), :])
            jm = jnp.maximum(jm, ref[part, k, pl.ds(8, 1), :])
        ll, jl = jnp.zeros_like(mm), jnp.zeros_like(jm)
        for k in range(8):
            ll += ref[part, k, pl.ds(4, 4), :] * jnp.exp2(ref[part, k, pl.ds(0, 4), :] - mm)
            jl += ref[part, k, pl.ds(9, 1), :] * jnp.exp2(ref[part, k, pl.ds(8, 1), :] - jm)
        return mm, ll, jm, jl

    def put(ref, part, values):
        for at_row, rows, v in zip((0, 4, 8, 9), (4, 4, 1, 1), values):
            ref[part, pl.ds(at_row, rows), :] = v

    def begin(copies):
        for cp in copies:
            cp.start()

    def finish(copies):
        for cp in copies:
            cp.wait()

    def swap(copies):
        begin(copies)
        finish(copies)

    class Stats:
        def __init__(self, part):
            self.part = part
            self.c1, self.c2, self.c3 = [], [], []
            for k in range(1, 8):
                p, dev = peer1(k)
                self.c1.append(remote(st.at[part, p], r1.at[part, g1], s1send.at[part, k], s1recv.at[part, k], dev))
                self.c3.append(remote(s3.at[part], r3.at[part, g1], s3send.at[part, k], s3recv.at[part, k], dev))
                p, dev = peer2(k)
                self.c2.append(remote(s2.at[part], r2.at[part, g2], s2send.at[part, k], s2recv.at[part, k], dev))

        def step1(self):
            r1[self.part, g1] = st[self.part, g1]
            begin(self.c1)

        def step2(self):
            finish(self.c1)
            put(s2, self.part, merged(r1, self.part))
            r2[self.part, g2] = s2[self.part]
            begin(self.c2)

        def step3(self):
            finish(self.c2)
            put(s3, self.part, merged(r2, self.part))
            r3[self.part, g1] = s3[self.part]
            begin(self.c3)

        def step4(self):
            finish(self.c3)
            for gi in range(8):
                st[self.part, gi, pl.ds(0, 4), :] = jnp.exp2(
                    st[self.part, gi, pl.ds(0, 4), :] - r3[self.part, gi, pl.ds(0, 4), :]
                ) / (r3[self.part, gi, pl.ds(4, 4), :] * 128.0)

    def index_stats():
        hcopy.wait()
        it = jnp.where(seen(), (ipart[...] + irecv[...]) * LOG2E, MASKED)
        im = jnp.max(it, axis=0, keepdims=True)
        il = jnp.sum(jnp.exp2(it - im), axis=0, keepdims=True)
        mis[...] = it
        for gi in range(8):
            st[0, gi, pl.ds(8, 1), :] = im
            st[0, gi, pl.ds(9, 1), :] = il

    st[...] = jnp.zeros_like(st)
    stats0, stats1 = Stats(0), Stats(1)

    lax.fori_loop(0, PAIRS // 2, prepare, 0, unroll=PUN)
    peak0 = scores(0, sc)

    def four_pairs(i, peak):
        peak2 = scores(2 * i + 1, sc2)
        powers(2 * i, sc, peak)
        nxt = scores(jnp.minimum(2 * i + 2, PAIRS // 2 - 1), sc)
        powers(2 * i + 1, sc2, peak2)

        @pl.when(i == 0)
        def _():
            p2.step3()

        @pl.when(i == 2)
        def _():
            p2.step4()
            widened(hst, 6144, 176, 96)
            lax.fori_loop(PAIRS // 2, PAIRS, prepare, 0, unroll=PUN)

        @pl.when(i == 3)
        def _():
            index_stats()
            stats0.step1()

        @pl.when(i == 4)
        def _():
            stats0.step2()

        @pl.when(i == 5)
        def _():
            stats0.step3()

        @pl.when(i == 7)
        def _():
            stats0.step4()

        return nxt

    lax.fori_loop(0, PAIRS // 4, four_pairs, peak0)

    def add_heads(part, ch, acc):
        def add_group(gi, acc):
            for a in range(2):
                pw = pm[part * 16 + gi * 2 + a, pl.ds(*CUTS[ch]), :].astype(F32)
                acc = acc + pw[:, :128] * st[part, gi, pl.ds(2 * a, 1), :]
                acc = acc + pw[:, 128:] * st[part, gi, pl.ds(2 * a + 1, 1), :]
            return acc

        return lax.fori_loop(0, 8, add_group, acc, unroll=4)

    def early(chs):
        for ch in chs:
            tpart[pl.ds(*CUTS[ch]), :] = add_heads(0, ch, jnp.zeros((CUTS[ch][1], QUERIES), F32))

    stats1.step1()
    early(range(0, 2))
    stats1.step2()
    early(range(2, CHUNKS))
    stats1.step3()
    gqt[...] = jnp.zeros_like(gqt)
    gwt[...] = jnp.zeros_like(gwt)
    jpeak, jtotal = s3[0, pl.ds(8, 1), :], s3[0, pl.ds(9, 1), :]
    stats1.step4()

    tcopies = []
    for ch in range(CHUNKS):
        rows = pl.ds(*CUTS[ch])
        tpart[rows, :] = add_heads(1, ch, tpart[rows, :])
        cp = remote(tpart.at[rows], trecv.at[rows], tsend.at[ch], trsem.at[ch], at(hd_=1 - hd))
        cp.start()
        tcopies.append(cp)

    kcopies = []
    for ch in range(CHUNKS):
        rows = pl.ds(*CUTS[ch])
        tcopies[ch].wait()
        predicted = jnp.exp2(mis[rows, :] - jpeak) / jtotal
        mis[rows, :] = (predicted - (tpart[rows, :] + trecv[rows, :])) * ALL_KEYS

        def slope_pair(jp, acc, rows=rows):
            iq = iqs[jp]
            mf = mis[rows, :]
            d = nt(key[rows, :], iq)
            parts = []
            for e in range(2):
                de = d[:, e * 128 : e * 128 + 128]
                gwt[pl.ds(2 * jp + e, 1), :] += jnp.sum(mf * jnp.maximum(de, 0.0), axis=0, keepdims=True)
                parts.append(jnp.where(de > 0, mf * wt[pl.ds(2 * jp + e, 1), :], 0.0).astype(BF16))
            sl = jnp.concatenate(parts, axis=1)
            gqt[jp] += nn(keyt[:, rows], sl)
            return acc + nn(sl, iq)

        gkp[rows, :] = lax.fori_loop(0, IPAIRS, slope_pair, jnp.zeros((CUTS[ch][1], IDIM), F32), unroll=UNR)
        cp = remote(gkp.at[rows], gkr.at[rows], ksend.at[ch], krsem.at[ch], at(hd_=1 - hd))
        cp.start()
        kcopies.append(cp)

    for j in range(IHEADS):
        tr = jnp.transpose(gqt[j // 2, :, pl.ds((j % 2) * 128, 128)])
        for r in range(2):
            rs[pl.ds(r * 32 + j, 64, stride=BR), :] = tr[r * 64 : r * 64 + 64]
    tw = jnp.transpose(gwt[...]) * INDEX_SCALE
    for r in range(16):
        rs[pl.ds(64 + r, 64, stride=BR), :] = tw[r * 64 : r * 64 + 64] if r < 2 else jnp.zeros((64, 128), F32)

    ccopy = remote(
        rs.at[pl.ds(pl.multiple_of((1 - c) * 32 * BR, BR), 32 * BR)], rcv, csend, crecv, other
    )
    ccopy.start()
    ccopy.wait()

    def add_core(o, _):
        oy, ox, oz = o // 8, lax.rem(o // 2, 4), lax.rem(o, 2)
        here = pl.ds(pl.multiple_of(o * BR, BR), BR)
        v = rcv[here, :] + rs[pl.ds(pl.multiple_of((c * 32 + o) * BR, BR), BR), :]
        rcv[here, :] = v
        w = v[64:72]
        low = w - w.astype(BF16).astype(F32)
        sb[oy, ox, oz] = jnp.concatenate([v[:72], low], axis=0).astype(BF16)
        return 0

    lax.fori_loop(0, 32, add_core, 0)
    cps = []
    for k in range(1, 4):
        yp, xp = lax.rem(y + k, 4), lax.rem(x + k, 4)
        cps.append(remote(sb.at[yp, four, 0], rya.at[k], ysend.at[k], yrecv.at[k], at(y_=yp)))
        cps.append(remote(sb.at[four, xp, 1], rxb.at[k], xsend.at[k], xrecv.at[k], at(x_=xp)))
    swap(cps)

    for o in range(4):
        for dest, src, index in (
            (0, rya, (y * 4 + o) * 2),
            (1, rxb, (o * 4 + x) * 2 + 1),
        ):
            v = rcv[pl.ds(pl.multiple_of(index * BR, BR), BR), :]
            main, w = v[:64], v[64:72]
            for k in range(1, 4):
                vk = src[k, o].astype(F32)
                main, w = main + vk[:64], w + (vk[64:72] + vk[72:])
            pab[dest, o, pl.ds(0, 64), :] = main
            pab[dest, o, pl.ds(64, 8), :] = w
            pab[dest, o, pl.ds(72, 8), :] = jnp.zeros((8, 128), F32)
    mine = x * (1 - zh) + y * zh
    theirs = x * zh + y * (1 - zh)
    rz[zh * 4 + mine] = pab[zh, mine]
    cps = []
    for k in range(1, 4):
        yp, xp = lax.rem(y + k, 4), lax.rem(x + k, 4)
        slot = zh * 4 + x
        cps.append(remote(pab.at[0, xp], rz.at[slot], zsend.at[k], zrecv.at[slot], at(zh_=0, x_=xp)))
        slot = zh * 4 + y
        cps.append(remote(pab.at[1, yp], rz.at[slot], zsend.at[3 + k], zrecv.at[slot], at(zh_=1, y_=yp)))
    slot = zh * 4 + theirs
    cps.append(remote(pab.at[1 - zh, theirs], rz.at[slot], zsend.at[0], zrecv.at[slot], across))
    begin(cps)
    for cp in cps:
        cp.wait_send()
    for k in range(1, 8):
        slot = lax.rem(zh * 4 + mine + k, 8)
        remote(pab.at[0, 0], rz.at[slot], zsend.at[0], zrecv.at[slot], across).wait_recv()
    total = rz[0]
    for k in range(1, 8):
        total = total + rz[k]
    raw[pl.ds(0, BR), :] = total
    for r in range(2):
        for j in range(IHEADS):
            gq_out[pl.ds(r, 1), pl.ds(j * 128, 128)] = raw[pl.ds(r * 32 + j, 1), :]
        gw_out[pl.ds(r, 1), :] = raw[pl.ds(64 + r, 1), pl.ds(0, IHEADS)]
    for cp in kcopies:
        cp.wait()
    gk_out[...] = gkp[...] + gkr[...]


def handed_on(*refs):
    count = len(refs) // 2
    for k in range(count):
        refs[count + k][...] = refs[k][...]


def shards(q_heads, w_uk, latent_t, index_query, index_key, head_weight, query_pos, key_start):
    vm = pl.BlockSpec(memory_space=pltpu.VMEM)
    dma = pltpu.SemaphoreType.DMA

    def v(*shape, dtype=F32):
        return pltpu.VMEM(shape, dtype)

    results = pl.pallas_call(
        body,
        out_shape=(
            jax.ShapeDtypeStruct((2, IHEADS * IDIM), F32),
            jax.ShapeDtypeStruct((KEYS, IDIM), F32),
            jax.ShapeDtypeStruct((2, IHEADS), F32),
        ),
        in_specs=[vm, vm, vm, vm, vm, pl.BlockSpec(memory_space=pl.ANY), vm, vm],
        out_specs=(vm, vm, vm),
        scratch_shapes=[
            v(272, 128),
            v(8, 128, dtype=jnp.int32),
            v(8, 128, dtype=jnp.int32),
            v(2, 4, 4, 2, 272, 128, dtype=BF16),
            v(2 * 64 * 96, 128),
            v(64 * 80, 128),
            v(HEADS, NOPE, 512, dtype=BF16),
            v(KEYS, 768, dtype=BF16),
            v(PAIRS, 256, 128, dtype=BF16),
            v(256, 128, dtype=BF16),
            v(KEYS, 512),
            v(KEYS, 512),
            v(PAIRS, KEYS, 256, dtype=BF16),
            v(IPAIRS, 256, 128, dtype=BF16),
            v(128, 128),
            v(KEYS, 128),
            v(KEYS, 128),
            v(2, 8, 16, 128),
            v(2, 8, 16, 128),
            v(2, 16, 128),
            v(2, 8, 16, 128),
            v(2, 16, 128),
            v(2, 8, 16, 128),
            v(KEYS, 128),
            v(KEYS, 128),
            v(KEYS, 128),
            v(128, KEYS, dtype=BF16),
            v(IPAIRS, 128, 256),
            v(128, 128),
            v(KEYS, 128),
            v(KEYS, 128),
            v(64 * BR, 128),
            v(32 * BR, 128),
            v(4, 4, 2, BR, 128, dtype=BF16),
            v(4, 4, BR, 128, dtype=BF16),
            v(4, 4, BR, 128, dtype=BF16),
            v(2, 4, BR, 128),
            v(8, BR, 128),
            dma, dma((NCOPY,)), dma((NCOPY,)), dma, dma,
            dma((CHUNKS,)), dma((CHUNKS,)), dma((CHUNKS,)), dma((CHUNKS,)),
            dma((2, 8)), dma((2, 8)), dma((2, 8)), dma((2, 8)), dma((2, 8)), dma((2, 8)),
            dma, dma, dma((4,)), dma((4,)), dma((4,)), dma((4,)),
            dma((8,)), dma((8,)),
        ],
        compiler_params=pltpu.CompilerParams(
            collective_id=0, has_side_effects=True, vmem_limit_bytes=63 * 1024 * 1024
        ),
    )(
        q_heads, index_query, head_weight, key_start.reshape(1, QUERIES), query_pos.reshape(1, QUERIES),
        w_uk, latent_t, index_key,
    )
    return pl.pallas_call(
        handed_on,
        out_shape=tuple(jax.ShapeDtypeStruct(v.shape, v.dtype) for v in results),
        in_specs=[vm] * 3,
        out_specs=(vm,) * 3,
    )(*results)


def solution(mesh):
    torus = Mesh(mesh.devices.reshape(2, 4, 4, 2, 2), AXES)
    placed = (
        P(CTX, "head"),
        P("head", None, None),
        P(None, CTX),
        P(CTX, "head"),
        P(CTX, None),
        P(CTX, "head"),
        P(),
        P(),
    )
    return jax.shard_map(
        shards,
        mesh=torus,
        in_specs=placed,
        out_specs=(P(CTX, "head"), P(CTX, None), P(CTX, "head")),
        check_vma=False,
    )
```
